32 devices in a mesh: grp: 2 (over y), space: 4 (over z), seg: 2 (over x), var: 2 (over core).
Axes of the slice: x: 2, y: 2, z: 4, core: 2. Of those that a mesh axis runs over, the one named last changes fastest.
Arguments:
- snapshots: bfloat16 [1024, 5, 2048], P(('grp', 'seg'), None, 'space'), parts along dimension 0, may hold values from -6 to 6
- weights: float32 [5, 4096], P(None, ('grp', 'space')), parts along dimension 1, may hold values from 0.4 to 10, as said below
- bins: int32 [32], replicated, may hold values from 1 to 127, as said below
Outputs:
- modes: float32 [32, 6, 5, 4096], P(('seg', 'var'), None, None, ('grp', 'space')), parts along dimension 3
- factor: float32 [64, 6, 6], P(('grp', 'seg', 'var')), parts along dimension 0
The draws below stay inside these ranges and needn't reach their ends.
There are 2 independent parts, one for each index of `grp`. The reference program is written for one: setup_inputs(seed, part) draws one part's arguments, and reference() takes and returns one part's arrays. A program takes and returns all parts, laid end to end along the dimension named above; an argument that names none is the same for every part. Nothing has to cross between parts.
Inputs may be any that keep to these rules, and one draw needn't show every extreme that they name: Positive quadrature weights. bins lie strictly between the zero bin and the Nyquist bin of a block.
All inputs are finite; a program needn't handle non-finite values.
Results may differ from the reference program's by a relative error of at most 0.0042.
Values may be sent and summed in bfloat16 or wider, within the bound.
A program may use at most 64 MiB of HBM per device.

```python
import math
import jax
import jax.numpy as jnp
from jax import lax

NV = 5
NF = 256
NFREQ = 32
HOP = 128
NB = 3
NT = 512
NCOL = 6
CELLS = 2048


def draw_weights(key, part):
    first = jax.random.fold_in(jax.random.fold_in(key, 11), 0)
    position = jnp.arange(CELLS, dtype=jnp.float32) / (CELLS - 1)
    rising = jnp.exp(jnp.log(3.0) * position)
    rough = jnp.exp(jax.random.uniform(first, (NV, CELLS), jnp.float32, jnp.log(0.5), jnp.log(2.0)))
    return (rising[None, :] * rough).astype(jnp.float32)


def draw_bins(key, part):
    first, second = jax.random.split(jax.random.fold_in(key, 23))
    values = jax.random.randint(first, (NFREQ,), 1, NF // 2, dtype=jnp.int32)
    order = jax.random.permutation(second, NFREQ)
    values = values.at[order[0]].set(1)
    values = values.at[order[1]].set(NF // 2 - 1)
    return values.astype(jnp.int32)


def steps_of(rng, extent, cuts, low, top_value):
    factor_of = 1.0
    for dim, shards_of in cuts:
        steps = jax.random.uniform(jax.random.fold_in(jax.random.fold_in(rng, 6), dim), (shards_of,), jnp.float32, low / len(cuts), top_value / len(cuts))
        factor_of = factor_of * jnp.repeat(jnp.exp(steps), extent[dim] // shards_of).reshape((-1,) + (1,) * (len(extent) - 1 - dim))
    return factor_of


def scatter_about(stream_key, shape, scale, most, cuts=(), kind=jnp.bfloat16):
    level = steps_of(stream_key, shape, cuts, -0.22, 0.18) if cuts else 1.0
    values = jax.random.normal(stream_key, shape, jnp.float32) * scale * level
    return jnp.minimum(jnp.maximum(values, -most), most).astype(kind)


def setup_inputs(seed: int = 0, part: int = 0) -> dict:
    arg_keys = jax.random.split(jax.random.key(seed), 4)
    own_keys = jax.random.split(jax.random.fold_in(arg_keys[3], part), 4)
    snapshots = scatter_about(own_keys[0], (NT, NV, CELLS), 1.0, 6.0, ((0, 2), (2, 4)))
    weights = draw_weights(jax.random.fold_in(jax.random.fold_in(arg_keys[3], part), 71), part)
    bins = draw_bins(jax.random.fold_in(arg_keys[3], 71), part)
    return dict(snapshots=snapshots, weights=weights, bins=bins)


def window_basis(offset, bin_index, length):
    phase = offset * bin_index % length
    angle = 2.0 * math.pi / length * phase.astype(jnp.float32)
    taper = 0.5 - 0.5 * jnp.cos(2.0 * math.pi / length * offset.astype(jnp.float32))
    factor = taper / math.sqrt(0.375 * length)
    return (factor * jnp.cos(angle), -factor * jnp.sin(angle))

def reference(snapshots, weights, bins):
    total_rows = NV * CELLS
    flat = snapshots.reshape(snapshots.shape[0], total_rows)
    offsets = jnp.arange(NF, dtype=jnp.int32)
    cosine, sine = window_basis(offsets[:, None], bins[None, :], NF)
    basis = jnp.stack([cosine, sine], 2).reshape(NF, 2 * NFREQ).astype(jnp.bfloat16)
    basis_t = basis.T

    def one_block(block):
        start = (block * HOP).astype(jnp.int32)
        frames = lax.dynamic_slice_in_dim(flat, start, NF, 0)
        return jnp.dot(basis_t.astype(jnp.float32), frames.astype(jnp.float32), preferred_element_type=jnp.float32).astype(jnp.bfloat16)
    blocks = lax.map(one_block, jnp.arange(NB, dtype=jnp.int32))
    blocks = blocks.reshape(NB, NFREQ, 2, total_rows)
    spectra = jnp.transpose(blocks, (1, 2, 0, 3)).reshape(NFREQ, NCOL, total_rows)
    flat_weights = weights.reshape(total_rows).astype(jnp.float32)
    identity = jnp.eye(NCOL, dtype=jnp.float32)

    def one_freq(matrix):
        values = matrix.astype(jnp.float32)
        gram = jnp.dot(values * flat_weights, values.T, precision=lax.Precision.HIGHEST) / (NV * CELLS)
        lower = jnp.linalg.cholesky(gram)
        inverse = jax.scipy.linalg.solve_triangular(lower, identity, lower=True)
        modes_one = jnp.dot(inverse, values, precision=lax.Precision.HIGHEST)
        return (modes_one, lower.T)
    modes, factor = lax.map(one_freq, spectra)
    return (modes.reshape(NFREQ, NCOL, NV, CELLS), factor)
```

```python
import functools
import math

import jax
import jax.numpy as jnp
from jax import lax
from jax.experimental import pallas as pl
from jax.experimental.pallas import tpu as pltpu
from jax.sharding import PartitionSpec as P


def window_basis(offset, bin_index, length):
    phase = offset * bin_index % length
    angle = 2.0 * math.pi / length * phase.astype(jnp.float32)
    taper = 0.5 - 0.5 * jnp.cos(2.0 * math.pi / length * offset.astype(jnp.float32))
    factor = taper / math.sqrt(0.375 * length)
    return (factor * jnp.cos(angle), -factor * jnp.sin(angle))


def invert_lower(lower):
    identity = jnp.eye(lower.shape[-1], dtype=lower.dtype)

    def solve_single(single):
        return jax.scipy.linalg.solve_triangular(single, identity, lower=True)

    return jax.vmap(solve_single)(lower)


MESH = pl.DeviceIdType.MESH


def cosine_of(phase, length):
    quarter = jnp.abs(phase - length // 2) - length // 4
    x = quarter.astype(jnp.float32) * (2.0 * math.pi / length)
    y = x * x
    poly = -1.0 / 39916800.0
    for term in (1.0 / 362880.0, -1.0 / 5040.0, 1.0 / 120.0, -1.0 / 6.0, 1.0):
        poly = poly * y + term
    return x * poly


def fill_basis(bins_ref, basis, frames, variables, seg, var, var_count):
    freq = 8
    columns = frames * 8
    lane = lax.broadcasted_iota(jnp.int32, (freq, columns), 1)
    row = lax.broadcasted_iota(jnp.int32, (freq, columns), 0)
    frame = lane >> 3
    slot = lane & 7
    taper = (0.5 - 0.5 * cosine_of(frame, frames)) / math.sqrt(0.375 * frames)
    half = columns // 2
    second = (lax.broadcasted_iota(jnp.int32, (2 * freq, columns), 1) >= half).astype(jnp.int32)
    overlap = second == 1 - seg
    slots = jnp.concatenate([slot, slot], 0)
    for group in range(2):
        owner = 1 - seg if group == 0 else seg
        first = (owner * var_count + var) * freq
        bin_of = jnp.zeros((freq, columns), jnp.int32)
        for f in range(freq):
            bin_of = jnp.where(row == f, bins_ref[first + f], bin_of)
        phase = (frame * bin_of) & (frames - 1)
        cosine = taper * cosine_of(phase, frames)
        sine = taper * cosine_of((phase + frames // 4) & (frames - 1), frames)
        whole = jnp.concatenate([cosine, sine], 0)
        shared = jnp.concatenate([whole[:, half:], whole[:, :half]], 1)
        shared = jnp.where(overlap, shared, 0.0)
        for kind, part in enumerate((whole, shared)):
            for v in range(variables):
                start = ((group * 2 + kind) * variables + v) * 2 * freq
                masked = jnp.where(slots == v, part, 0.0)
                basis[pl.ds(start, 2 * freq), :] = masked.astype(jnp.bfloat16)


def kernel(space_count, var_count, x_hbm, w_ref, bins_ref, modes_ref, factor_ref,
           x_vmem, padded, basis, values, own_half, send_a, send_h, recv_a, recv_h, gram_buf,
           x_sem, a_send_sem, a_recv_sem, h_send_sem, h_recv_sem, g_send_sem, g_recv_sem):
    frames, variables, cells = x_hbm.shape
    freq = 8
    chunks, rows, width = send_a.shape
    seg = lax.axis_index("seg")
    var = lax.axis_index("var")
    me = lax.axis_index("space")
    other = 1 - seg
    pieces = x_sem.shape[0]
    step = frames // pieces
    loads = []
    for k in range(pieces):
        load = pltpu.make_async_copy(
            x_hbm.at[pl.ds(k * step, step)], x_vmem.at[pl.ds(k * step, step)], x_sem.at[k])
        load.start()
        loads.append(load)

    barrier = pltpu.get_barrier_semaphore()
    pl.semaphore_signal(barrier, inc=1, device_id={"seg": other}, device_id_type=MESH)
    for d in range(1, space_count):
        pl.semaphore_signal(
            barrier, inc=1, device_id={"space": lax.rem(me + d, space_count)}, device_id_type=MESH)

    fill_basis(bins_ref, basis, frames, variables, seg, var, var_count)

    for k in range(pieces):
        loads[k].wait()
        block = x_vmem[pl.ds(k * step, step)].astype(jnp.float32)
        block = jnp.concatenate([block, jnp.zeros((step, 8 - variables, cells), jnp.float32)], 1)
        padded[pl.ds(k * step * 8, step * 8), :] = block.reshape(step * 8, cells).astype(jnp.bfloat16)

    pl.semaphore_wait(barrier, space_count)

    a_copies, h_copies = [], []
    for c in range(chunks):
        lanes = pl.ds(c * width, width)
        summed = jnp.dot(basis[...], padded[:, lanes], preferred_element_type=jnp.float32)
        send_a[c] = summed[:rows].astype(send_a.dtype)
        send_h[c] = summed[rows:2 * rows].astype(send_h.dtype)
        for src, dst, ssem, rsem, copies in (
            (send_h, recv_h, h_send_sem, h_recv_sem, h_copies),
            (send_a, recv_a, a_send_sem, a_recv_sem, a_copies),
        ):
            copy = pltpu.make_async_remote_copy(
                src_ref=src.at[c], dst_ref=dst.at[c], send_sem=ssem.at[c], recv_sem=rsem.at[c],
                device_id={"seg": other}, device_id_type=MESH)
            copy.start()
            copies.append(copy)
        own = summed[2 * rows:3 * rows].astype(jnp.bfloat16).astype(jnp.float32)
        own_half[:, lanes] = summed[3 * rows:]
        for v in range(variables):
            for part in range(2):
                start = (v * 2 + part) * freq
                values[3 * part + 2 * seg, v, :, lanes] = own[start:start + freq]

    columns = 6
    pairs = [(i, j) for i in range(columns) for j in range(i + 1)]
    sums = [None] * len(pairs)
    for c in range(chunks):
        lanes = pl.ds(c * width, width)
        h_copies[c].wait_recv()
        total = own_half[:, lanes] + recv_h[c].astype(jnp.float32)
        total = total.astype(jnp.bfloat16).astype(jnp.float32)
        a_copies[c].wait_recv()
        far = recv_a[c].astype(jnp.float32)
        for v in range(variables):
            for part in range(2):
                start = (v * 2 + part) * freq
                values[3 * part + 1, v, :, lanes] = total[start:start + freq]
                values[3 * part + 2 * other, v, :, lanes] = far[start:start + freq]
        for v in range(variables):
            for at in range(c * width, (c + 1) * width, 128):
                one = pl.ds(at, 128)
                weight = jnp.broadcast_to(w_ref[v:v + 1, one], (freq, 128))
                plain = [values[i, v, :, one] for i in range(columns)]
                scaled = [p * weight for p in plain]
                for n, (i, j) in enumerate(pairs):
                    term = scaled[i] * plain[j]
                    sums[n] = term if sums[n] is None else sums[n] + term

    lane = lax.broadcasted_iota(jnp.int32, (freq, 128), 1)
    packed = jnp.zeros((freq, 128), jnp.float32)
    for n in range(len(pairs)):
        packed = jnp.where(lane == n, jnp.sum(sums[n], axis=1, keepdims=True), packed)
    gram_buf[me] = packed
    g_copies = []
    for d in range(1, space_count):
        copy = pltpu.make_async_remote_copy(
            src_ref=gram_buf.at[me], dst_ref=gram_buf.at[me],
            send_sem=g_send_sem.at[d - 1], recv_sem=g_recv_sem.at[d - 1],
            device_id={"space": lax.rem(me + d, space_count)}, device_id_type=MESH)
        copy.start()
        g_copies.append(copy)
    for copy in g_copies:
        copy.wait_recv()
    gram = gram_buf[0]
    for d in range(1, space_count):
        gram = gram + gram_buf[d]
    gram = gram * (1.0 / (variables * cells * space_count))
    entry = {
        pair: jnp.broadcast_to(gram[:, n:n + 1], (freq, 128)) for n, pair in enumerate(pairs)}

    lower, inverse = {}, {}
    for j in range(columns):
        rest = entry[j, j]
        for k in range(j):
            rest = rest - lower[j, k] * lower[j, k]
        inverse[j, j] = lax.rsqrt(rest)
        lower[j, j] = rest * inverse[j, j]
        for i in range(j + 1, columns):
            rest = entry[i, j]
            for k in range(j):
                rest = rest - lower[i, k] * lower[j, k]
            lower[i, j] = rest * inverse[j, j]
    for j in range(columns):
        for i in range(j + 1, columns):
            total = lower[i, j] * inverse[j, j]
            for k in range(j + 1, i):
                total = total + lower[i, k] * inverse[k, j]
            inverse[i, j] = -total * inverse[i, i]

    for i in range(columns):
        line = jnp.zeros((freq, 128), jnp.float32)
        for j in range(i, columns):
            line = jnp.where(lane == j, lower[j, i], line)
        factor_ref[i] = line

    for v in range(variables):
        for at in range(0, cells, 128):
            one = pl.ds(at, 128)
            plain = [values[i, v, :, one] for i in range(columns)]
            for i in range(columns):
                mode = inverse[i, 0] * plain[0]
                for j in range(1, i + 1):
                    mode = mode + inverse[i, j] * plain[j]
                modes_ref[i, v, :, one] = mode

    for copy in a_copies + h_copies + g_copies:
        copy.wait_send()


def on_device_kernel(snapshots, weights, bins):
    frames, variables, cells = snapshots.shape
    space_count = lax.axis_size("space")
    freq, columns, chunks = 8, 6, 2
    width = cells // chunks
    rows = variables * 2 * freq
    half_type = jnp.float32
    dma = pltpu.SemaphoreType.DMA
    modes, factor = pl.pallas_call(
        functools.partial(kernel, space_count, lax.axis_size("var")),
        out_shape=(
            jax.ShapeDtypeStruct((columns, variables, freq, cells), jnp.float32),
            jax.ShapeDtypeStruct((columns, freq, 128), jnp.float32),
        ),
        in_specs=[
            pl.BlockSpec(memory_space=pl.ANY),
            pl.BlockSpec(memory_space=pltpu.VMEM),
            pl.BlockSpec(memory_space=pltpu.SMEM),
        ],
        out_specs=(pl.BlockSpec(memory_space=pltpu.VMEM),) * 2,
        scratch_shapes=[
            pltpu.VMEM((frames, variables, cells), jnp.bfloat16),
            pltpu.VMEM((frames * 8, cells), jnp.bfloat16),
            pltpu.VMEM((4 * rows, frames * 8), jnp.bfloat16),
            pltpu.VMEM((columns, variables, freq, cells), jnp.float32),
            pltpu.VMEM((rows, cells), jnp.float32),
            pltpu.VMEM((chunks, rows, width), jnp.bfloat16),
            pltpu.VMEM((chunks, rows, width), half_type),
            pltpu.VMEM((chunks, rows, width), jnp.bfloat16),
            pltpu.VMEM((chunks, rows, width), half_type),
            pltpu.VMEM((space_count, freq, 128), jnp.float32),
            dma((8,)),
            dma((chunks,)), dma((chunks,)), dma((chunks,)), dma((chunks,)),
            dma((space_count - 1,)), dma((space_count - 1,)),
        ],
        compiler_params=pltpu.CompilerParams(
            collective_id=0, has_side_effects=True, vmem_limit_bytes=40 * 1024 * 1024),
    )(snapshots, weights, bins)
    return jnp.transpose(modes, (2, 0, 1, 3)), jnp.transpose(factor[:, :, :columns], (1, 0, 2))


def on_device(snapshots, weights, bins):
    seg_count = lax.axis_size("seg")
    var_count = lax.axis_size("var")
    space_count = lax.axis_size("space")
    frames, variables, cell_dev = snapshots.shape
    flat_rows = variables * cell_dev
    hop_len = frames // 2
    block_count = 2 * seg_count - 1
    freq_dev = bins.shape[0] // (seg_count * var_count)
    own = snapshots.reshape(frames, flat_rows)
    start_bin = (lax.axis_index("seg") * var_count + lax.axis_index("var")) * freq_dev
    chosen = lax.dynamic_slice_in_dim(bins, start_bin, freq_dev)
    piece = lax.all_gather(own, "seg", axis=0, tiled=True)
    count = piece.shape[0]
    moments = jnp.arange(count, dtype=jnp.int32)
    offset = moments[:, None] - hop_len * jnp.arange(block_count, dtype=jnp.int32)[None, :]
    inside = (offset >= 0) & (offset < frames)
    safe_offset = jnp.where(inside, offset, 0)
    cosine, sine = window_basis(safe_offset[:, :, None], chosen[None, None, :], frames)
    coeffs = jnp.stack([cosine, sine], 3) * inside[:, :, None, None].astype(jnp.float32)
    coeffs = jnp.transpose(coeffs, (0, 2, 3, 1)).reshape(count, freq_dev * 2 * block_count)
    coeffs = coeffs.astype(jnp.bfloat16)
    summed = jnp.einsum("pk,pr->kr", coeffs, piece, preferred_element_type=jnp.float32)
    spectra = summed.astype(jnp.bfloat16).reshape(freq_dev, 2 * block_count, flat_rows)
    values = spectra.astype(jnp.float32)
    scaled = values * weights.reshape(flat_rows)
    local_gram = jnp.einsum("fir,fjr->fij", scaled, values, precision=lax.Precision.HIGHEST)
    local_gram = local_gram / (variables * cell_dev * space_count)
    lower = jnp.linalg.cholesky(lax.psum(local_gram, "space"))
    inverse = invert_lower(lower)
    modes = jnp.einsum("fij,fjr->fir", inverse, values, precision=lax.Precision.HIGHEST)
    modes = modes.reshape(freq_dev, 2 * block_count, variables, cell_dev)
    return (modes, jnp.swapaxes(lower, 1, 2))


def per_device(snapshots, weights, bins):
    seg_count = lax.axis_size("seg")
    frames, variables, cells = snapshots.shape
    freq_dev = bins.shape[0] // (seg_count * lax.axis_size("var"))
    fits = seg_count == 2 and freq_dev == 8 and variables <= 8 and cells % 256 == 0
    fits = fits and frames >= 64 and frames & (frames - 1) == 0 and lax.axis_size("space") > 1
    return (on_device_kernel if fits else on_device)(snapshots, weights, bins)


def solution(mesh):
    return jax.shard_map(
        per_device,
        mesh=mesh,
        in_specs=(P(("grp", "seg"), None, "space"), P(None, ("grp", "space")), P()),
        out_specs=(
            P(("seg", "var"), None, None, ("grp", "space")),
            P(("grp", "seg", "var"), None, None),
        ),
        check_vma=False,
    )
```

```python
import functools
import math

import jax
import jax.numpy as jnp
from jax import lax
from jax.experimental import pallas as pl
from jax.experimental.pallas import tpu as pltpu
from jax.sharding import PartitionSpec as P


def window_basis(offset, bin_index, length):
    phase = offset * bin_index % length
    angle = 2.0 * math.pi / length * phase.astype(jnp.float32)
    taper = 0.5 - 0.5 * jnp.cos(2.0 * math.pi / length * offset.astype(jnp.float32))
    factor = taper / math.sqrt(0.375 * length)
    return (factor * jnp.cos(angle), -factor * jnp.sin(angle))


def invert_lower(lower):
    identity = jnp.eye(lower.shape[-1], dtype=lower.dtype)

    def solve_single(single):
        return jax.scipy.linalg.solve_triangular(single, identity, lower=True)

    return jax.vmap(solve_single)(lower)


MESH = pl.DeviceIdType.MESH


def cosine_of(phase, length):
    quarter = jnp.abs(phase - length // 2) - length // 4
    x = quarter.astype(jnp.float32) * (2.0 * math.pi / length)
    y = x * x
    poly = -1.0 / 39916800.0
    for term in (1.0 / 362880.0, -1.0 / 5040.0, 1.0 / 120.0, -1.0 / 6.0, 1.0):
        poly = poly * y + term
    return x * poly


def basis_rows(bins_ref, frames, seg, var, var_count):
    freq = 8
    shape = (freq, frames)
    frame = lax.broadcasted_iota(jnp.int32, shape, 1)
    row = lax.broadcasted_iota(jnp.int32, shape, 0)
    half = frames // 2
    taper = (0.5 - 0.5 * cosine_of(frame, frames)) / math.sqrt(0.375 * frames)
    second = (lax.broadcasted_iota(jnp.int32, (2 * freq, frames), 1) >= half).astype(jnp.int32)
    overlap = second == 1 - seg
    rows = []
    for group in range(2):
        owner = 1 - seg if group == 0 else seg
        first = (owner * var_count + var) * freq
        bin_of = jnp.zeros(shape, jnp.int32)
        for f in range(freq):
            bin_of = jnp.where(row == f, bins_ref[first + f], bin_of)
        phase = (frame * bin_of) & (frames - 1)
        cosine = taper * cosine_of(phase, frames)
        sine = taper * cosine_of((phase + frames // 4) & (frames - 1), frames)
        whole = jnp.concatenate([cosine, sine], 0)
        shared = jnp.concatenate([whole[:, half:], whole[:, :half]], 1)
        rows += [whole, jnp.where(overlap, shared, 0.0)]
    return jnp.concatenate(rows, 0).astype(jnp.bfloat16)


def kernel(space_count, var_count, x_hbm, w_hbm, bins_hbm, modes_ref, factor_ref,
           x_vmem, w_ref, bins_ref, values, own_half, send_a, send_h, recv_a, recv_h, gram_buf,
           x_sem, w_sem, bins_sem, a_send_sem, a_recv_sem, h_send_sem, h_recv_sem, g_send_sem, g_recv_sem):
    variables, frames, cells = x_hbm.shape
    freq = 8
    rows = 2 * freq
    seg = lax.axis_index("seg")
    var = lax.axis_index("var")
    me = lax.axis_index("space")
    other = 1 - seg
    bins_load = pltpu.make_async_copy(bins_hbm, bins_ref, bins_sem)
    bins_load.start()
    loads = []
    for v in range(variables):
        load = pltpu.make_async_copy(x_hbm.at[v], x_vmem.at[v], x_sem.at[v])
        load.start()
        loads.append(load)

    w_load = pltpu.make_async_copy(w_hbm, w_ref, w_sem)
    w_load.start()

    barrier = pltpu.get_barrier_semaphore()
    pl.semaphore_signal(barrier, inc=1, device_id={"seg": other}, device_id_type=MESH)
    for d in range(1, space_count):
        pl.semaphore_signal(
            barrier, inc=1, device_id={"space": lax.rem(me + d, space_count)}, device_id_type=MESH)

    bins_load.wait()
    basis = basis_rows(bins_ref, frames, seg, var, var_count)
    pl.semaphore_wait(barrier, space_count)

    a_copies, h_copies = [], []
    for v in range(variables):
        loads[v].wait()
        summed = jnp.dot(basis, x_vmem[v], preferred_element_type=jnp.float32)
        send_h[v] = summed[rows:2 * rows].astype(send_h.dtype)
        send_a[v] = summed[:rows].astype(send_a.dtype)
        for src, dst, ssem, rsem, copies in (
            (send_h, recv_h, h_send_sem, h_recv_sem, h_copies),
            (send_a, recv_a, a_send_sem, a_recv_sem, a_copies),
        ):
            copy = pltpu.make_async_remote_copy(
                src_ref=src.at[v], dst_ref=dst.at[v], send_sem=ssem.at[v], recv_sem=rsem.at[v],
                device_id={"seg": other}, device_id_type=MESH)
            copy.start()
            copies.append(copy)
        own = summed[2 * rows:3 * rows].astype(jnp.bfloat16).astype(jnp.float32)
        own_half[v] = summed[3 * rows:]
        for part in range(2):
            values[3 * part + 2 * seg, v] = own[part * freq:(part + 1) * freq]

    w_load.wait()
    columns = 6
    pairs = [(i, j) for i in range(columns) for j in range(i + 1)]
    sums = [None] * len(pairs)
    for v in range(variables):
        h_copies[v].wait_recv()
        total = own_half[v] + recv_h[v].astype(jnp.float32)
        total = total.astype(jnp.bfloat16).astype(jnp.float32)
        a_copies[v].wait_recv()
        far = recv_a[v].astype(jnp.float32)
        for part in range(2):
            values[3 * part + 1, v] = total[part * freq:(part + 1) * freq]
            values[3 * part + 2 * other, v] = far[part * freq:(part + 1) * freq]
        for at in range(0, cells, 128):
            one = pl.ds(at, 128)
            weight = jnp.broadcast_to(w_ref[v:v + 1, one], (freq, 128))
            plain = [values[i, v, :, one] for i in range(columns)]
            scaled = [p * weight for p in plain]
            for n, (i, j) in enumerate(pairs):
                term = scaled[i] * plain[j]
                sums[n] = term if sums[n] is None else sums[n] + term

    lane = lax.broadcasted_iota(jnp.int32, (freq, 128), 1)
    packed = jnp.zeros((freq, 128), jnp.float32)
    for n in range(len(pairs)):
        packed = jnp.where(lane == n, jnp.sum(sums[n], axis=1, keepdims=True), packed)
    gram_buf[me] = packed
    g_copies = []
    for d in range(1, space_count):
        copy = pltpu.make_async_remote_copy(
            src_ref=gram_buf.at[me], dst_ref=gram_buf.at[me],
            send_sem=g_send_sem.at[d - 1], recv_sem=g_recv_sem.at[d - 1],
            device_id={"space": lax.rem(me + d, space_count)}, device_id_type=MESH)
        copy.start()
        g_copies.append(copy)
    for copy in g_copies:
        copy.wait_recv()
    gram = gram_buf[0]
    for d in range(1, space_count):
        gram = gram + gram_buf[d]
    gram = gram * (1.0 / (variables * cells * space_count))
    entry = {
        pair: jnp.broadcast_to(gram[:, n:n + 1], (freq, 128)) for n, pair in enumerate(pairs)}

    lower, inverse = {}, {}
    for j in range(columns):
        rest = entry[j, j]
        for k in range(j):
            rest = rest - lower[j, k] * lower[j, k]
        inverse[j, j] = lax.rsqrt(rest)
        lower[j, j] = rest * inverse[j, j]
        for i in range(j + 1, columns):
            rest = entry[i, j]
            for k in range(j):
                rest = rest - lower[i, k] * lower[j, k]
            lower[i, j] = rest * inverse[j, j]
    for j in range(columns):
        for i in range(j + 1, columns):
            total = lower[i, j] * inverse[j, j]
            for k in range(j + 1, i):
                total = total + lower[i, k] * inverse[k, j]
            inverse[i, j] = -total * inverse[i, i]

    for i in range(columns):
        line = jnp.zeros((freq, 128), jnp.float32)
        for j in range(i, columns):
            line = jnp.where(lane == j, lower[j, i], line)
        factor_ref[i] = line[:, :columns]

    for v in range(variables):
        for at in range(0, cells, 128):
            one = pl.ds(at, 128)
            plain = [values[i, v, :, one] for i in range(columns)]
            for i in range(columns):
                mode = inverse[i, 0] * plain[0]
                for j in range(1, i + 1):
                    mode = mode + inverse[i, j] * plain[j]
                modes_ref[i, v, :, one] = mode

    for copy in a_copies + h_copies + g_copies:
        copy.wait_send()


def on_device_kernel(snapshots, weights, bins):
    frames, variables, cells = snapshots.shape
    space_count = lax.axis_size("space")
    freq, columns = 8, 6
    rows = 2 * freq
    dma = pltpu.SemaphoreType.DMA
    modes, factor = pl.pallas_call(
        functools.partial(kernel, space_count, lax.axis_size("var")),
        out_shape=(
            jax.ShapeDtypeStruct((columns, variables, freq, cells), jnp.float32),
            jax.ShapeDtypeStruct((columns, freq, columns), jnp.float32),
        ),
        in_specs=[
            pl.BlockSpec(memory_space=pltpu.HBM),
            pl.BlockSpec(memory_space=pltpu.HBM),
            pl.BlockSpec(memory_space=pltpu.HBM),
        ],
        out_specs=(pl.BlockSpec(memory_space=pltpu.VMEM),) * 2,
        scratch_shapes=[
            pltpu.VMEM((variables, frames, cells), jnp.bfloat16),
            pltpu.VMEM((variables, cells), jnp.float32),
            pltpu.SMEM(bins.shape, jnp.int32),
            pltpu.VMEM((columns, variables, freq, cells), jnp.float32),
            pltpu.VMEM((variables, rows, cells), jnp.float32),
            pltpu.VMEM((variables, rows, cells), jnp.bfloat16),
            pltpu.VMEM((variables, rows, cells), jnp.float32),
            pltpu.VMEM((variables, rows, cells), jnp.bfloat16),
            pltpu.VMEM((variables, rows, cells), jnp.float32),
            pltpu.VMEM((space_count, freq, 128), jnp.float32),
            dma((variables,)), dma, dma,
            dma((variables,)), dma((variables,)), dma((variables,)), dma((variables,)),
            dma((space_count - 1,)), dma((space_count - 1,)),
        ],
        compiler_params=pltpu.CompilerParams(
            collective_id=0, has_side_effects=True, vmem_limit_bytes=64 * 1024 * 1024),
    )(jnp.transpose(snapshots, (1, 0, 2)), weights, bins)
    return jnp.transpose(modes, (2, 0, 1, 3)), jnp.transpose(factor, (1, 0, 2))


def on_device(snapshots, weights, bins):
    seg_count = lax.axis_size("seg")
    var_count = lax.axis_size("var")
    space_count = lax.axis_size("space")
    frames, variables, cell_dev = snapshots.shape
    flat_rows = variables * cell_dev
    hop_len = frames // 2
    block_count = 2 * seg_count - 1
    freq_dev = bins.shape[0] // (seg_count * var_count)
    own = snapshots.reshape(frames, flat_rows)
    start_bin = (lax.axis_index("seg") * var_count + lax.axis_index("var")) * freq_dev
    chosen = lax.dynamic_slice_in_dim(bins, start_bin, freq_dev)
    piece = lax.all_gather(own, "seg", axis=0, tiled=True)
    count = piece.shape[0]
    moments = jnp.arange(count, dtype=jnp.int32)
    offset = moments[:, None] - hop_len * jnp.arange(block_count, dtype=jnp.int32)[None, :]
    inside = (offset >= 0) & (offset < frames)
    safe_offset = jnp.where(inside, offset, 0)
    cosine, sine = window_basis(safe_offset[:, :, None], chosen[None, None, :], frames)
    coeffs = jnp.stack([cosine, sine], 3) * inside[:, :, None, None].astype(jnp.float32)
    coeffs = jnp.transpose(coeffs, (0, 2, 3, 1)).reshape(count, freq_dev * 2 * block_count)
    coeffs = coeffs.astype(jnp.bfloat16)
    summed = jnp.einsum("pk,pr->kr", coeffs, piece, preferred_element_type=jnp.float32)
    spectra = summed.astype(jnp.bfloat16).reshape(freq_dev, 2 * block_count, flat_rows)
    values = spectra.astype(jnp.float32)
    scaled = values * weights.reshape(flat_rows)
    local_gram = jnp.einsum("fir,fjr->fij", scaled, values, precision=lax.Precision.HIGHEST)
    local_gram = local_gram / (variables * cell_dev * space_count)
    lower = jnp.linalg.cholesky(lax.psum(local_gram, "space"))
    inverse = invert_lower(lower)
    modes = jnp.einsum("fij,fjr->fir", inverse, values, precision=lax.Precision.HIGHEST)
    modes = modes.reshape(freq_dev, 2 * block_count, variables, cell_dev)
    return (modes, jnp.swapaxes(lower, 1, 2))


def per_device(snapshots, weights, bins):
    seg_count = lax.axis_size("seg")
    frames, variables, cells = snapshots.shape
    freq_dev = bins.shape[0] // (seg_count * lax.axis_size("var"))
    fits = seg_count == 2 and freq_dev == 8 and cells % 128 == 0
    fits = fits and frames >= 256 and frames & (frames - 1) == 0 and lax.axis_size("space") > 1
    return (on_device_kernel if fits else on_device)(snapshots, weights, bins)


def solution(mesh):
    return jax.shard_map(
        per_device,
        mesh=mesh,
        in_specs=(P(("grp", "seg"), None, "space"), P(None, ("grp", "space")), P()),
        out_specs=(
            P(("seg", "var"), None, None, ("grp", "space")),
            P(("grp", "seg", "var"), None, None),
        ),
        check_vma=False,
    )
```

```python
import functools
import math

import jax
import jax.numpy as jnp
from jax import lax
from jax.experimental import pallas as pl
from jax.experimental.pallas import tpu as pltpu
from jax.sharding import PartitionSpec as P


def window_basis(offset, bin_index, length):
    phase = offset * bin_index % length
    angle = 2.0 * math.pi / length * phase.astype(jnp.float32)
    taper = 0.5 - 0.5 * jnp.cos(2.0 * math.pi / length * offset.astype(jnp.float32))
    factor = taper / math.sqrt(0.375 * length)
    return (factor * jnp.cos(angle), -factor * jnp.sin(angle))


def invert_lower(lower):
    identity = jnp.eye(lower.shape[-1], dtype=lower.dtype)

    def solve_single(single):
        return jax.scipy.linalg.solve_triangular(single, identity, lower=True)

    return jax.vmap(solve_single)(lower)


MESH = pl.DeviceIdType.MESH


def cosine_of(phase, length):
    quarter = jnp.abs(phase - length // 2) - length // 4
    x = quarter.astype(jnp.float32) * (2.0 * math.pi / length)
    y = x * x
    poly = -1.0 / 39916800.0
    for term in (1.0 / 362880.0, -1.0 / 5040.0, 1.0 / 120.0, -1.0 / 6.0, 1.0):
        poly = poly * y + term
    return x * poly


def basis_rows(bins_ref, frames, seg, var, var_count):
    freq = 8
    shape = (freq, frames)
    frame = lax.broadcasted_iota(jnp.int32, shape, 1)
    row = lax.broadcasted_iota(jnp.int32, shape, 0)
    half = frames // 2
    taper = (0.5 - 0.5 * cosine_of(frame, frames)) / math.sqrt(0.375 * frames)
    second = (lax.broadcasted_iota(jnp.int32, (2 * freq, frames), 1) >= half).astype(jnp.int32)
    overlap = second == 1 - seg
    rows = []
    for group in range(2):
        owner = 1 - seg if group == 0 else seg
        first = (owner * var_count + var) * freq
        bin_of = jnp.zeros(shape, jnp.int32)
        for f in range(freq):
            bin_of = jnp.where(row == f, bins_ref[first + f], bin_of)
        phase = (frame * bin_of) & (frames - 1)
        cosine = taper * cosine_of(phase, frames)
        sine = taper * cosine_of((phase + frames // 4) & (frames - 1), frames)
        whole = jnp.concatenate([cosine, sine], 0)
        shared = jnp.concatenate([whole[:, half:], whole[:, :half]], 1)
        rows += [whole, jnp.where(overlap, shared, 0.0)]
    return jnp.concatenate(rows, 0).astype(jnp.bfloat16)


def kernel(space_count, var_count, x_hbm, w_hbm, bins_hbm, values, gram_ref,
           x_vmem, w_ref, bins_ref, own_half, send_a, send_h, recv_a, recv_h, gram_buf,
           x_sem, w_sem, bins_sem, a_send_sem, a_recv_sem, h_send_sem, h_recv_sem, g_send_sem, g_recv_sem):
    variables, frames, cells = x_hbm.shape
    freq = 8
    rows = 2 * freq
    seg = lax.axis_index("seg")
    var = lax.axis_index("var")
    me = lax.axis_index("space")
    other = 1 - seg
    bins_load = pltpu.make_async_copy(bins_hbm, bins_ref, bins_sem)
    bins_load.start()
    loads = []
    for v in range(variables):
        load = pltpu.make_async_copy(x_hbm.at[v], x_vmem.at[v], x_sem.at[v])
        load.start()
        loads.append(load)

    w_load = pltpu.make_async_copy(w_hbm, w_ref, w_sem)
    w_load.start()

    barrier = pltpu.get_barrier_semaphore()
    pl.semaphore_signal(barrier, inc=1, device_id={"seg": other}, device_id_type=MESH)
    for d in range(1, space_count):
        pl.semaphore_signal(
            barrier, inc=1, device_id={"space": lax.rem(me + d, space_count)}, device_id_type=MESH)

    bins_load.wait()
    basis = basis_rows(bins_ref, frames, seg, var, var_count)
    pl.semaphore_wait(barrier, space_count)

    a_copies, h_copies = [], []
    for v in range(variables):
        loads[v].wait()
        summed = jnp.dot(basis, x_vmem[v], preferred_element_type=jnp.float32)
        send_h[v] = summed[rows:2 * rows].astype(send_h.dtype)
        send_a[v] = summed[:rows].astype(send_a.dtype)
        for src, dst, ssem, rsem, copies in (
            (send_h, recv_h, h_send_sem, h_recv_sem, h_copies),
            (send_a, recv_a, a_send_sem, a_recv_sem, a_copies),
        ):
            copy = pltpu.make_async_remote_copy(
                src_ref=src.at[v], dst_ref=dst.at[v], send_sem=ssem.at[v], recv_sem=rsem.at[v],
                device_id={"seg": other}, device_id_type=MESH)
            copy.start()
            copies.append(copy)
        own = summed[2 * rows:3 * rows].astype(jnp.bfloat16).astype(jnp.float32)
        own_half[v] = summed[3 * rows:]
        for part in range(2):
            values[3 * part + 2 * seg, v] = own[part * freq:(part + 1) * freq]

    w_load.wait()
    columns = 6
    pairs = [(i, j) for i in range(columns) for j in range(i + 1)]
    sums = [None] * len(pairs)
    for v in range(variables):
        h_copies[v].wait_recv()
        total = own_half[v] + recv_h[v].astype(jnp.float32)
        total = total.astype(jnp.bfloat16).astype(jnp.float32)
        a_copies[v].wait_recv()
        far = recv_a[v].astype(jnp.float32)
        for part in range(2):
            values[3 * part + 1, v] = total[part * freq:(part + 1) * freq]
            values[3 * part + 2 * other, v] = far[part * freq:(part + 1) * freq]
        for at in range(0, cells, 128):
            one = pl.ds(at, 128)
            weight = jnp.broadcast_to(w_ref[v:v + 1, one], (freq, 128))
            plain = [values[i, v, :, one] for i in range(columns)]
            scaled = [p * weight for p in plain]
            for n, (i, j) in enumerate(pairs):
                term = scaled[i] * plain[j]
                sums[n] = term if sums[n] is None else sums[n] + term

    lane = lax.broadcasted_iota(jnp.int32, (freq, 128), 1)
    packed = jnp.zeros((freq, 128), jnp.float32)
    for n in range(len(pairs)):
        packed = jnp.where(lane == n, jnp.sum(sums[n], axis=1, keepdims=True), packed)
    gram_buf[me] = packed
    g_copies = []
    for d in range(1, space_count):
        copy = pltpu.make_async_remote_copy(
            src_ref=gram_buf.at[me], dst_ref=gram_buf.at[me],
            send_sem=g_send_sem.at[d - 1], recv_sem=g_recv_sem.at[d - 1],
            device_id={"space": lax.rem(me + d, space_count)}, device_id_type=MESH)
        copy.start()
        g_copies.append(copy)
    for copy in g_copies:
        copy.wait_recv()
    gram = gram_buf[0]
    for d in range(1, space_count):
        gram = gram + gram_buf[d]
    gram_ref[...] = gram

    for copy in a_copies + h_copies + g_copies:
        copy.wait_send()


def modes_kernel(space_count, values, gram_ref, modes_hbm, factor_ref, modes_vmem, modes_sem):
    columns, variables, freq, cells = values.shape
    pairs = [(i, j) for i in range(columns) for j in range(i + 1)]
    lane = lax.broadcasted_iota(jnp.int32, (freq, 128), 1)
    gram = gram_ref[...] * (1.0 / (variables * cells * space_count))
    entry = {
        pair: jnp.broadcast_to(gram[:, n:n + 1], (freq, 128)) for n, pair in enumerate(pairs)}

    lower, inverse = {}, {}
    for j in range(columns):
        rest = entry[j, j]
        for k in range(j):
            rest = rest - lower[j, k] * lower[j, k]
        inverse[j, j] = lax.rsqrt(rest)
        lower[j, j] = rest * inverse[j, j]
        for i in range(j + 1, columns):
            rest = entry[i, j]
            for k in range(j):
                rest = rest - lower[i, k] * lower[j, k]
            lower[i, j] = rest * inverse[j, j]
    for j in range(columns):
        for i in range(j + 1, columns):
            total = lower[i, j] * inverse[j, j]
            for k in range(j + 1, i):
                total = total + lower[i, k] * inverse[k, j]
            inverse[i, j] = -total * inverse[i, i]

    for i in range(columns):
        line = jnp.zeros((freq, 128), jnp.float32)
        for j in range(i, columns):
            line = jnp.where(lane == j, lower[j, i], line)
        factor_ref[i] = line[:, :columns]

    copies = []
    for i in range(columns):
        for v in range(variables):
            for at in range(0, cells, 128):
                one = pl.ds(at, 128)
                mode = inverse[i, 0] * values[0, v, :, one]
                for j in range(1, i + 1):
                    mode = mode + inverse[i, j] * values[j, v, :, one]
                modes_vmem[i, v, :, one] = mode
        copy = pltpu.make_async_copy(modes_vmem.at[i], modes_hbm.at[i], modes_sem.at[i])
        copy.start()
        copies.append(copy)
    for copy in copies:
        copy.wait()


def on_device_kernel(snapshots, weights, bins):
    frames, variables, cells = snapshots.shape
    space_count = lax.axis_size("space")
    freq, columns = 8, 6
    rows = 2 * freq
    dma = pltpu.SemaphoreType.DMA
    inputs = [jnp.transpose(snapshots, (1, 0, 2)), weights, bins]
    inputs = [pltpu.with_memory_space_constraint(value, pltpu.HBM) for value in inputs]
    values, gram = pl.pallas_call(
        functools.partial(kernel, space_count, lax.axis_size("var")),
        out_shape=(
            jax.ShapeDtypeStruct((columns, variables, freq, cells), jnp.float32),
            jax.ShapeDtypeStruct((freq, 128), jnp.float32),
        ),
        in_specs=[
            pl.BlockSpec(memory_space=pltpu.HBM),
            pl.BlockSpec(memory_space=pltpu.HBM),
            pl.BlockSpec(memory_space=pltpu.HBM),
        ],
        out_specs=(pl.BlockSpec(memory_space=pltpu.VMEM),) * 2,
        scratch_shapes=[
            pltpu.VMEM((variables, frames, cells), jnp.bfloat16),
            pltpu.VMEM((variables, cells), jnp.float32),
            pltpu.SMEM(bins.shape, jnp.int32),
            pltpu.VMEM((variables, rows, cells), jnp.float32),
            pltpu.VMEM((variables, rows, cells), jnp.bfloat16),
            pltpu.VMEM((variables, rows, cells), jnp.float32),
            pltpu.VMEM((variables, rows, cells), jnp.bfloat16),
            pltpu.VMEM((variables, rows, cells), jnp.float32),
            pltpu.VMEM((space_count, freq, 128), jnp.float32),
            dma((variables,)), dma, dma,
            dma((variables,)), dma((variables,)), dma((variables,)), dma((variables,)),
            dma((space_count - 1,)), dma((space_count - 1,)),
        ],
        compiler_params=pltpu.CompilerParams(
            collective_id=0, has_side_effects=True, vmem_limit_bytes=32 * 1024 * 1024),
    )(*inputs)
    modes, factor = pl.pallas_call(
        functools.partial(modes_kernel, space_count),
        out_shape=(
            jax.ShapeDtypeStruct((columns, variables, freq, cells), jnp.float32),
            jax.ShapeDtypeStruct((columns, freq, columns), jnp.float32),
        ),
        in_specs=[pl.BlockSpec(memory_space=pltpu.VMEM)] * 2,
        out_specs=(pl.BlockSpec(memory_space=pltpu.HBM), pl.BlockSpec(memory_space=pltpu.VMEM)),
        scratch_shapes=[
            pltpu.VMEM((columns, variables, freq, cells), jnp.float32),
            dma((columns,)),
        ],
        compiler_params=pltpu.CompilerParams(vmem_limit_bytes=16 * 1024 * 1024),
    )(values, gram)
    return jnp.transpose(modes, (2, 0, 1, 3)), jnp.transpose(factor, (1, 0, 2))


def on_device(snapshots, weights, bins):
    seg_count = lax.axis_size("seg")
    var_count = lax.axis_size("var")
    space_count = lax.axis_size("space")
    frames, variables, cell_dev = snapshots.shape
    flat_rows = variables * cell_dev
    hop_len = frames // 2
    block_count = 2 * seg_count - 1
    freq_dev = bins.shape[0] // (seg_count * var_count)
    own = snapshots.reshape(frames, flat_rows)
    start_bin = (lax.axis_index("seg") * var_count + lax.axis_index("var")) * freq_dev
    chosen = lax.dynamic_slice_in_dim(bins, start_bin, freq_dev)
    piece = lax.all_gather(own, "seg", axis=0, tiled=True)
    count = piece.shape[0]
    moments = jnp.arange(count, dtype=jnp.int32)
    offset = moments[:, None] - hop_len * jnp.arange(block_count, dtype=jnp.int32)[None, :]
    inside = (offset >= 0) & (offset < frames)
    safe_offset = jnp.where(inside, offset, 0)
    cosine, sine = window_basis(safe_offset[:, :, None], chosen[None, None, :], frames)
    coeffs = jnp.stack([cosine, sine], 3) * inside[:, :, None, None].astype(jnp.float32)
    coeffs = jnp.transpose(coeffs, (0, 2, 3, 1)).reshape(count, freq_dev * 2 * block_count)
    coeffs = coeffs.astype(jnp.bfloat16)
    summed = jnp.einsum("pk,pr->kr", coeffs, piece, preferred_element_type=jnp.float32)
    spectra = summed.astype(jnp.bfloat16).reshape(freq_dev, 2 * block_count, flat_rows)
    values = spectra.astype(jnp.float32)
    scaled = values * weights.reshape(flat_rows)
    local_gram = jnp.einsum("fir,fjr->fij", scaled, values, precision=lax.Precision.HIGHEST)
    local_gram = local_gram / (variables * cell_dev * space_count)
    lower = jnp.linalg.cholesky(lax.psum(local_gram, "space"))
    inverse = invert_lower(lower)
    modes = jnp.einsum("fij,fjr->fir", inverse, values, precision=lax.Precision.HIGHEST)
    modes = modes.reshape(freq_dev, 2 * block_count, variables, cell_dev)
    return (modes, jnp.swapaxes(lower, 1, 2))


def per_device(snapshots, weights, bins):
    seg_count = lax.axis_size("seg")
    frames, variables, cells = snapshots.shape
    freq_dev = bins.shape[0] // (seg_count * lax.axis_size("var"))
    fits = seg_count == 2 and freq_dev == 8 and cells % 128 == 0
    fits = fits and frames >= 256 and frames & (frames - 1) == 0 and lax.axis_size("space") > 1
    return (on_device_kernel if fits else on_device)(snapshots, weights, bins)


def solution(mesh):
    return jax.shard_map(
        per_device,
        mesh=mesh,
        in_specs=(P(("grp", "seg"), None, "space"), P(None, ("grp", "space")), P()),
        out_specs=(
            P(("seg", "var"), None, None, ("grp", "space")),
            P(("grp", "seg", "var"), None, None),
        ),
        check_vma=False,
    )
```

```python
import functools
import math

import jax
import jax.numpy as jnp
from jax import lax
from jax.experimental import pallas as pl
from jax.experimental.pallas import tpu as pltpu
from jax.sharding import PartitionSpec as P


def window_basis(offset, bin_index, length):
    phase = offset * bin_index % length
    angle = 2.0 * math.pi / length * phase.astype(jnp.float32)
    taper = 0.5 - 0.5 * jnp.cos(2.0 * math.pi / length * offset.astype(jnp.float32))
    factor = taper / math.sqrt(0.375 * length)
    return (factor * jnp.cos(angle), -factor * jnp.sin(angle))


def invert_lower(lower):
    identity = jnp.eye(lower.shape[-1], dtype=lower.dtype)

    def solve_single(single):
        return jax.scipy.linalg.solve_triangular(single, identity, lower=True)

    return jax.vmap(solve_single)(lower)


MESH = pl.DeviceIdType.MESH


def cosine_of(phase, length):
    quarter = jnp.abs(phase - length // 2) - length // 4
    x = quarter.astype(jnp.float32) * (2.0 * math.pi / length)
    y = x * x
    poly = -1.0 / 39916800.0
    for term in (1.0 / 362880.0, -1.0 / 5040.0, 1.0 / 120.0, -1.0 / 6.0, 1.0):
        poly = poly * y + term
    return x * poly


def basis_rows(bins_ref, frames, seg, var, var_count):
    freq = 8
    shape = (freq, frames)
    frame = lax.broadcasted_iota(jnp.int32, shape, 1)
    row = lax.broadcasted_iota(jnp.int32, shape, 0)
    half = frames // 2
    taper = (0.5 - 0.5 * cosine_of(frame, frames)) / math.sqrt(0.375 * frames)
    second = (lax.broadcasted_iota(jnp.int32, (2 * freq, frames), 1) >= half).astype(jnp.int32)
    overlap = second == 1 - seg
    rows = []
    for group in range(2):
        owner = 1 - seg if group == 0 else seg
        first = (owner * var_count + var) * freq
        bin_of = jnp.zeros(shape, jnp.int32)
        for f in range(freq):
            bin_of = jnp.where(row == f, bins_ref[first + f], bin_of)
        phase = (frame * bin_of) & (frames - 1)
        cosine = taper * cosine_of(phase, frames)
        sine = taper * cosine_of((phase + frames // 4) & (frames - 1), frames)
        whole = jnp.concatenate([cosine, sine], 0)
        shared = jnp.concatenate([whole[:, half:], whole[:, :half]], 1)
        rows += [whole, jnp.where(overlap, shared, 0.0)]
    return jnp.concatenate(rows, 0).astype(jnp.bfloat16)


def kernel(space_count, var_count, x_hbm, w_hbm, bins_hbm, values, gram_ref,
           x_vmem, w_ref, bins_ref, own_half, send, recv, gram_buf,
           x_sem, w_sem, bins_sem, send_sem, recv_sem, g_send_sem, g_recv_sem):
    variables, frames, cells = x_hbm.shape
    freq = 8
    rows = 2 * freq
    seg = lax.axis_index("seg")
    var = lax.axis_index("var")
    me = lax.axis_index("space")
    other = 1 - seg
    bins_load = pltpu.make_async_copy(bins_hbm, bins_ref, bins_sem)
    bins_load.start()
    loads = []
    for v in range(variables):
        load = pltpu.make_async_copy(x_hbm.at[v], x_vmem.at[v], x_sem.at[v])
        load.start()
        loads.append(load)

    w_load = pltpu.make_async_copy(w_hbm, w_ref, w_sem)
    w_load.start()

    barrier = pltpu.get_barrier_semaphore()
    pl.semaphore_signal(barrier, inc=1, device_id={"seg": other}, device_id_type=MESH)
    for d in range(1, space_count):
        pl.semaphore_signal(
            barrier, inc=1, device_id={"space": lax.rem(me + d, space_count)}, device_id_type=MESH)

    bins_load.wait()
    basis = basis_rows(bins_ref, frames, seg, var, var_count)
    pl.semaphore_wait(barrier, space_count)

    copies = []
    for v in range(variables):
        loads[v].wait()
        summed = jnp.dot(basis, x_vmem[v], preferred_element_type=jnp.float32)
        send[v] = summed[:2 * rows].astype(send.dtype)
        copy = pltpu.make_async_remote_copy(
            src_ref=send.at[v], dst_ref=recv.at[v], send_sem=send_sem.at[v], recv_sem=recv_sem.at[v],
            device_id={"seg": other}, device_id_type=MESH)
        copy.start()
        copies.append(copy)
        own = summed[2 * rows:3 * rows].astype(jnp.bfloat16).astype(jnp.float32)
        own_half[v] = summed[3 * rows:]
        for part in range(2):
            values[3 * part + 2 * seg, v] = own[part * freq:(part + 1) * freq]

    w_load.wait()
    columns = 6
    pairs = [(i, j) for i in range(columns) for j in range(i + 1)]
    sums = [None] * len(pairs)
    for v in range(variables):
        copies[v].wait_recv()
        far = recv[v].astype(jnp.float32)
        total = own_half[v] + far[rows:]
        total = total.astype(jnp.bfloat16).astype(jnp.float32)
        for part in range(2):
            values[3 * part + 1, v] = total[part * freq:(part + 1) * freq]
            values[3 * part + 2 * other, v] = far[part * freq:(part + 1) * freq]
        for at in range(0, cells, 128):
            one = pl.ds(at, 128)
            weight = jnp.broadcast_to(w_ref[v:v + 1, one], (freq, 128))
            plain = [values[i, v, :, one] for i in range(columns)]
            scaled = [p * weight for p in plain]
            for n, (i, j) in enumerate(pairs):
                term = scaled[i] * plain[j]
                sums[n] = term if sums[n] is None else sums[n] + term

    lane = lax.broadcasted_iota(jnp.int32, (freq, 128), 1)
    packed = jnp.zeros((freq, 128), jnp.float32)
    for n in range(len(pairs)):
        packed = jnp.where(lane == n, jnp.sum(sums[n], axis=1, keepdims=True), packed)
    gram_buf[me] = packed
    g_copies = []
    for d in range(1, space_count):
        copy = pltpu.make_async_remote_copy(
            src_ref=gram_buf.at[me], dst_ref=gram_buf.at[me],
            send_sem=g_send_sem.at[d - 1], recv_sem=g_recv_sem.at[d - 1],
            device_id={"space": lax.rem(me + d, space_count)}, device_id_type=MESH)
        copy.start()
        g_copies.append(copy)
    for copy in g_copies:
        copy.wait_recv()
    gram = gram_buf[0]
    for d in range(1, space_count):
        gram = gram + gram_buf[d]
    gram_ref[...] = gram

    for copy in copies + g_copies:
        copy.wait_send()


def modes_kernel(space_count, values, gram_ref, modes_hbm, factor_ref, modes_vmem, modes_sem):
    columns, variables, freq, cells = values.shape
    pairs = [(i, j) for i in range(columns) for j in range(i + 1)]
    lane = lax.broadcasted_iota(jnp.int32, (freq, 128), 1)
    gram = gram_ref[...] * (1.0 / (variables * cells * space_count))
    entry = {
        pair: jnp.broadcast_to(gram[:, n:n + 1], (freq, 128)) for n, pair in enumerate(pairs)}

    lower, inverse = {}, {}
    for j in range(columns):
        rest = entry[j, j]
        for k in range(j):
            rest = rest - lower[j, k] * lower[j, k]
        inverse[j, j] = lax.rsqrt(rest)
        lower[j, j] = rest * inverse[j, j]
        for i in range(j + 1, columns):
            rest = entry[i, j]
            for k in range(j):
                rest = rest - lower[i, k] * lower[j, k]
            lower[i, j] = rest * inverse[j, j]
    for j in range(columns):
        for i in range(j + 1, columns):
            total = lower[i, j] * inverse[j, j]
            for k in range(j + 1, i):
                total = total + lower[i, k] * inverse[k, j]
            inverse[i, j] = -total * inverse[i, i]

    for i in range(columns):
        line = jnp.zeros((freq, 128), jnp.float32)
        for j in range(i, columns):
            line = jnp.where(lane == j, lower[j, i], line)
        factor_ref[i] = line[:, :columns]

    copies = []
    for i in range(columns):
        for v in range(variables):
            for at in range(0, cells, 128):
                one = pl.ds(at, 128)
                mode = inverse[i, 0] * values[0, v, :, one]
                for j in range(1, i + 1):
                    mode = mode + inverse[i, j] * values[j, v, :, one]
                modes_vmem[i, v, :, one] = mode
        copy = pltpu.make_async_copy(modes_vmem.at[i], modes_hbm.at[i], modes_sem.at[i])
        copy.start()
        copies.append(copy)
    for copy in copies:
        copy.wait()


def on_device_kernel(snapshots, weights, bins):
    frames, variables, cells = snapshots.shape
    space_count = lax.axis_size("space")
    freq, columns = 8, 6
    rows = 2 * freq
    dma = pltpu.SemaphoreType.DMA
    inputs = [jnp.transpose(snapshots, (1, 0, 2)), weights, bins]
    inputs = [pltpu.with_memory_space_constraint(value, pltpu.HBM) for value in inputs]
    values, gram = pl.pallas_call(
        functools.partial(kernel, space_count, lax.axis_size("var")),
        out_shape=(
            jax.ShapeDtypeStruct((columns, variables, freq, cells), jnp.float32),
            jax.ShapeDtypeStruct((freq, 128), jnp.float32),
        ),
        in_specs=[
            pl.BlockSpec(memory_space=pltpu.HBM),
            pl.BlockSpec(memory_space=pltpu.HBM),
            pl.BlockSpec(memory_space=pltpu.HBM),
        ],
        out_specs=(pl.BlockSpec(memory_space=pltpu.VMEM),) * 2,
        scratch_shapes=[
            pltpu.VMEM((variables, frames, cells), jnp.bfloat16),
            pltpu.VMEM((variables, cells), jnp.float32),
            pltpu.SMEM(bins.shape, jnp.int32),
            pltpu.VMEM((variables, rows, cells), jnp.float32),
            pltpu.VMEM((variables, 2 * rows, cells), jnp.bfloat16),
            pltpu.VMEM((variables, 2 * rows, cells), jnp.bfloat16),
            pltpu.VMEM((space_count, freq, 128), jnp.float32),
            dma((variables,)), dma, dma,
            dma((variables,)), dma((variables,)),
            dma((space_count - 1,)), dma((space_count - 1,)),
        ],
        compiler_params=pltpu.CompilerParams(
            collective_id=0, has_side_effects=True, vmem_limit_bytes=32 * 1024 * 1024),
    )(*inputs)
    modes, factor = pl.pallas_call(
        functools.partial(modes_kernel, space_count),
        out_shape=(
            jax.ShapeDtypeStruct((columns, variables, freq, cells), jnp.float32),
            jax.ShapeDtypeStruct((columns, freq, columns), jnp.float32),
        ),
        in_specs=[pl.BlockSpec(memory_space=pltpu.VMEM)] * 2,
        out_specs=(pl.BlockSpec(memory_space=pltpu.HBM), pl.BlockSpec(memory_space=pltpu.VMEM)),
        scratch_shapes=[
            pltpu.VMEM((columns, variables, freq, cells), jnp.float32),
            dma((columns,)),
        ],
        compiler_params=pltpu.CompilerParams(vmem_limit_bytes=16 * 1024 * 1024),
    )(values, gram)
    return jnp.transpose(modes, (2, 0, 1, 3)), jnp.transpose(factor, (1, 0, 2))


def on_device(snapshots, weights, bins):
    seg_count = lax.axis_size("seg")
    var_count = lax.axis_size("var")
    space_count = lax.axis_size("space")
    frames, variables, cell_dev = snapshots.shape
    flat_rows = variables * cell_dev
    hop_len = frames // 2
    block_count = 2 * seg_count - 1
    freq_dev = bins.shape[0] // (seg_count * var_count)
    own = snapshots.reshape(frames, flat_rows)
    start_bin = (lax.axis_index("seg") * var_count + lax.axis_index("var")) * freq_dev
    chosen = lax.dynamic_slice_in_dim(bins, start_bin, freq_dev)
    piece = lax.all_gather(own, "seg", axis=0, tiled=True)
    count = piece.shape[0]
    moments = jnp.arange(count, dtype=jnp.int32)
    offset = moments[:, None] - hop_len * jnp.arange(block_count, dtype=jnp.int32)[None, :]
    inside = (offset >= 0) & (offset < frames)
    safe_offset = jnp.where(inside, offset, 0)
    cosine, sine = window_basis(safe_offset[:, :, None], chosen[None, None, :], frames)
    coeffs = jnp.stack([cosine, sine], 3) * inside[:, :, None, None].astype(jnp.float32)
    coeffs = jnp.transpose(coeffs, (0, 2, 3, 1)).reshape(count, freq_dev * 2 * block_count)
    coeffs = coeffs.astype(jnp.bfloat16)
    summed = jnp.einsum("pk,pr->kr", coeffs, piece, preferred_element_type=jnp.float32)
    spectra = summed.astype(jnp.bfloat16).reshape(freq_dev, 2 * block_count, flat_rows)
    values = spectra.astype(jnp.float32)
    scaled = values * weights.reshape(flat_rows)
    local_gram = jnp.einsum("fir,fjr->fij", scaled, values, precision=lax.Precision.HIGHEST)
    local_gram = local_gram / (variables * cell_dev * space_count)
    lower = jnp.linalg.cholesky(lax.psum(local_gram, "space"))
    inverse = invert_lower(lower)
    modes = jnp.einsum("fij,fjr->fir", inverse, values, precision=lax.Precision.HIGHEST)
    modes = modes.reshape(freq_dev, 2 * block_count, variables, cell_dev)
    return (modes, jnp.swapaxes(lower, 1, 2))


def per_device(snapshots, weights, bins):
    seg_count = lax.axis_size("seg")
    frames, variables, cells = snapshots.shape
    freq_dev = bins.shape[0] // (seg_count * lax.axis_size("var"))
    fits = seg_count == 2 and freq_dev == 8 and cells % 128 == 0
    fits = fits and frames >= 256 and frames & (frames - 1) == 0 and lax.axis_size("space") > 1
    return (on_device_kernel if fits else on_device)(snapshots, weights, bins)


def solution(mesh):
    return jax.shard_map(
        per_device,
        mesh=mesh,
        in_specs=(P(("grp", "seg"), None, "space"), P(None, ("grp", "space")), P()),
        out_specs=(
            P(("seg", "var"), None, None, ("grp", "space")),
            P(("grp", "seg", "var"), None, None),
        ),
        check_vma=False,
    )
```

```python
import functools
import math

import jax
import jax.numpy as jnp
from jax import lax
from jax.experimental import pallas as pl
from jax.experimental.pallas import tpu as pltpu
from jax.sharding import PartitionSpec as P


def window_basis(offset, bin_index, length):
    phase = offset * bin_index % length
    angle = 2.0 * math.pi / length * phase.astype(jnp.float32)
    taper = 0.5 - 0.5 * jnp.cos(2.0 * math.pi / length * offset.astype(jnp.float32))
    factor = taper / math.sqrt(0.375 * length)
    return (factor * jnp.cos(angle), -factor * jnp.sin(angle))


def invert_lower(lower):
    identity = jnp.eye(lower.shape[-1], dtype=lower.dtype)

    def solve_single(single):
        return jax.scipy.linalg.solve_triangular(single, identity, lower=True)

    return jax.vmap(solve_single)(lower)


MESH = pl.DeviceIdType.MESH


def cosine_of(phase, length):
    quarter = jnp.abs(phase - length // 2) - length // 4
    x = quarter.astype(jnp.float32) * (2.0 * math.pi / length)
    y = x * x
    poly = -1.0 / 39916800.0
    for term in (1.0 / 362880.0, -1.0 / 5040.0, 1.0 / 120.0, -1.0 / 6.0, 1.0):
        poly = poly * y + term
    return x * poly


def basis_rows(bins_ref, frames, seg, var, var_count):
    freq = 8
    shape = (freq, frames)
    frame = lax.broadcasted_iota(jnp.int32, shape, 1)
    row = lax.broadcasted_iota(jnp.int32, shape, 0)
    half = frames // 2
    taper = (0.5 - 0.5 * cosine_of(frame, frames)) / math.sqrt(0.375 * frames)
    second = (lax.broadcasted_iota(jnp.int32, (2 * freq, frames), 1) >= half).astype(jnp.int32)
    overlap = second == 1 - seg
    rows = []
    for group in range(2):
        owner = 1 - seg if group == 0 else seg
        first = (owner * var_count + var) * freq
        bin_of = jnp.zeros(shape, jnp.int32)
        for f in range(freq):
            bin_of = jnp.where(row == f, bins_ref[first + f], bin_of)
        phase = (frame * bin_of) & (frames - 1)
        cosine = taper * cosine_of(phase, frames)
        sine = taper * cosine_of((phase + frames // 4) & (frames - 1), frames)
        whole = jnp.concatenate([cosine, sine], 0)
        shared = jnp.concatenate([whole[:, half:], whole[:, :half]], 1)
        rows += [whole, jnp.where(overlap, shared, 0.0)]
    return jnp.concatenate(rows, 0).astype(jnp.bfloat16)


def kernel(space_count, var_count, x_hbm, w_hbm, bins_hbm, values, gram_ref,
           x_vmem, w_ref, bins_ref, own_half, send, recv, gram_buf,
           x_sem, w_sem, bins_sem, send_sem, recv_sem, g_send_sem, g_recv_sem, turn_sem):
    variables, frames, cells = x_hbm.shape
    freq = 8
    rows = 2 * freq
    seg = lax.axis_index("seg")
    var = lax.axis_index("var")
    me = lax.axis_index("space")
    other = 1 - seg
    bins_load = pltpu.make_async_copy(bins_hbm, bins_ref, bins_sem)
    bins_load.start()
    loads = []
    for v in range(variables):
        load = pltpu.make_async_copy(x_hbm.at[v], x_vmem.at[v], x_sem.at[v])
        load.start()
        loads.append(load)

    w_load = pltpu.make_async_copy(w_hbm, w_ref, w_sem)
    w_load.start()

    barrier = pltpu.get_barrier_semaphore()
    pl.semaphore_signal(barrier, inc=1, device_id={"seg": other}, device_id_type=MESH)
    pl.semaphore_signal(barrier, inc=1, device_id={"var": 1 - var}, device_id_type=MESH)
    for d in range(1, space_count):
        pl.semaphore_signal(
            barrier, inc=1, device_id={"space": lax.rem(me + d, space_count)}, device_id_type=MESH)

    bins_load.wait()
    basis = basis_rows(bins_ref, frames, seg, var, var_count)
    pl.semaphore_wait(barrier, space_count + 1)

    copies = []
    for v in range(variables):
        loads[v].wait()
        summed = jnp.dot(basis, x_vmem[v], preferred_element_type=jnp.float32)
        send[v] = summed[:2 * rows].astype(send.dtype)
        copy = pltpu.make_async_remote_copy(
            src_ref=send.at[v], dst_ref=recv.at[v], send_sem=send_sem.at[v], recv_sem=recv_sem.at[v],
            device_id={"seg": other}, device_id_type=MESH)
        pl.when(var == 0)(copy.start)
        copies.append(copy)
        own = summed[2 * rows:3 * rows].astype(jnp.bfloat16).astype(jnp.float32)
        own_half[v] = summed[3 * rows:]
        for part in range(2):
            values[3 * part + 2 * seg, v] = own[part * freq:(part + 1) * freq]

    early = 3

    @pl.when(var == 0)
    def _():
        for copy in copies[:early]:
            copy.wait_send()
        pl.semaphore_signal(turn_sem, inc=1, device_id={"var": 1 - var}, device_id_type=MESH)

    @pl.when(var != 0)
    def _():
        pl.semaphore_wait(turn_sem, 1)
        for copy in copies:
            copy.start()

    w_load.wait()
    columns = 6
    pairs = [(i, j) for i in range(columns) for j in range(i + 1)]
    sums = [None] * len(pairs)
    for v in range(variables):
        copies[v].wait_recv()
        far = recv[v].astype(jnp.float32)
        total = own_half[v] + far[rows:]
        total = total.astype(jnp.bfloat16).astype(jnp.float32)
        for part in range(2):
            values[3 * part + 1, v] = total[part * freq:(part + 1) * freq]
            values[3 * part + 2 * other, v] = far[part * freq:(part + 1) * freq]
        for at in range(0, cells, 128):
            one = pl.ds(at, 128)
            weight = jnp.broadcast_to(w_ref[v:v + 1, one], (freq, 128))
            plain = [values[i, v, :, one] for i in range(columns)]
            scaled = [p * weight for p in plain]
            for n, (i, j) in enumerate(pairs):
                term = scaled[i] * plain[j]
                sums[n] = term if sums[n] is None else sums[n] + term

    lane = lax.broadcasted_iota(jnp.int32, (freq, 128), 1)
    packed = jnp.zeros((freq, 128), jnp.float32)
    for n in range(len(pairs)):
        packed = jnp.where(lane == n, jnp.sum(sums[n], axis=1, keepdims=True), packed)
    gram_buf[me] = packed
    g_copies = []
    for d in range(1, space_count):
        copy = pltpu.make_async_remote_copy(
            src_ref=gram_buf.at[me], dst_ref=gram_buf.at[me],
            send_sem=g_send_sem.at[d - 1], recv_sem=g_recv_sem.at[d - 1],
            device_id={"space": lax.rem(me + d, space_count)}, device_id_type=MESH)
        copy.start()
        g_copies.append(copy)
    for copy in g_copies:
        copy.wait_recv()
    gram = gram_buf[0]
    for d in range(1, space_count):
        gram = gram + gram_buf[d]
    gram_ref[...] = gram

    @pl.when(var != 0)
    def _():
        for copy in copies[:early]:
            copy.wait_send()

    for copy in copies[early:] + g_copies:
        copy.wait_send()


def modes_kernel(space_count, values, gram_ref, modes_hbm, factor_hbm, modes_vmem, factor_ref, modes_sem, factor_sem):
    columns, variables, freq, cells = values.shape
    pairs = [(i, j) for i in range(columns) for j in range(i + 1)]
    lane = lax.broadcasted_iota(jnp.int32, (freq, 128), 1)
    gram = gram_ref[...] * (1.0 / (variables * cells * space_count))
    entry = {
        pair: jnp.broadcast_to(gram[:, n:n + 1], (freq, 128)) for n, pair in enumerate(pairs)}

    lower, inverse = {}, {}
    for j in range(columns):
        rest = entry[j, j]
        for k in range(j):
            rest = rest - lower[j, k] * lower[j, k]
        inverse[j, j] = lax.rsqrt(rest)
        lower[j, j] = rest * inverse[j, j]
        for i in range(j + 1, columns):
            rest = entry[i, j]
            for k in range(j):
                rest = rest - lower[i, k] * lower[j, k]
            lower[i, j] = rest * inverse[j, j]
    for j in range(columns):
        for i in range(j + 1, columns):
            total = lower[i, j] * inverse[j, j]
            for k in range(j + 1, i):
                total = total + lower[i, k] * inverse[k, j]
            inverse[i, j] = -total * inverse[i, i]

    for i in range(columns):
        line = jnp.zeros((freq, 128), jnp.float32)
        for j in range(i, columns):
            line = jnp.where(lane == j, lower[j, i], line)
        factor_ref[i] = line[:, :columns]

    copies = [pltpu.make_async_copy(factor_ref, factor_hbm, factor_sem)]
    copies[0].start()
    for i in range(columns):
        for v in range(variables):
            for at in range(0, cells, 128):
                one = pl.ds(at, 128)
                mode = inverse[i, 0] * values[0, v, :, one]
                for j in range(1, i + 1):
                    mode = mode + inverse[i, j] * values[j, v, :, one]
                modes_vmem[i, v, :, one] = mode
        copy = pltpu.make_async_copy(modes_vmem.at[i], modes_hbm.at[i], modes_sem.at[i])
        copy.start()
        copies.append(copy)
    for copy in copies:
        copy.wait()


def on_device_kernel(snapshots, weights, bins):
    frames, variables, cells = snapshots.shape
    space_count = lax.axis_size("space")
    freq, columns = 8, 6
    rows = 2 * freq
    dma = pltpu.SemaphoreType.DMA
    inputs = [jnp.transpose(snapshots, (1, 0, 2)), weights, bins]
    inputs = [pltpu.with_memory_space_constraint(value, pltpu.HBM) for value in inputs]
    values, gram = pl.pallas_call(
        functools.partial(kernel, space_count, lax.axis_size("var")),
        out_shape=(
            jax.ShapeDtypeStruct((columns, variables, freq, cells), jnp.float32),
            jax.ShapeDtypeStruct((freq, 128), jnp.float32),
        ),
        in_specs=[
            pl.BlockSpec(memory_space=pltpu.HBM),
            pl.BlockSpec(memory_space=pltpu.HBM),
            pl.BlockSpec(memory_space=pltpu.HBM),
        ],
        out_specs=(pl.BlockSpec(memory_space=pltpu.VMEM),) * 2,
        scratch_shapes=[
            pltpu.VMEM((variables, frames, cells), jnp.bfloat16),
            pltpu.VMEM((variables, cells), jnp.float32),
            pltpu.SMEM(bins.shape, jnp.int32),
            pltpu.VMEM((variables, rows, cells), jnp.float32),
            pltpu.VMEM((variables, 2 * rows, cells), jnp.bfloat16),
            pltpu.VMEM((variables, 2 * rows, cells), jnp.bfloat16),
            pltpu.VMEM((space_count, freq, 128), jnp.float32),
            dma((variables,)), dma, dma,
            dma((variables,)), dma((variables,)),
            dma((space_count - 1,)), dma((space_count - 1,)),
            pltpu.SemaphoreType.REGULAR,
        ],
        compiler_params=pltpu.CompilerParams(
            collective_id=0, has_side_effects=True, vmem_limit_bytes=32 * 1024 * 1024),
    )(*inputs)
    modes, factor = pl.pallas_call(
        functools.partial(modes_kernel, space_count),
        out_shape=(
            jax.ShapeDtypeStruct((columns, variables, freq, cells), jnp.float32),
            jax.ShapeDtypeStruct((columns, freq, columns), jnp.float32),
        ),
        in_specs=[pl.BlockSpec(memory_space=pltpu.VMEM)] * 2,
        out_specs=(pl.BlockSpec(memory_space=pltpu.HBM),) * 2,
        scratch_shapes=[
            pltpu.VMEM((columns, variables, freq, cells), jnp.float32),
            pltpu.VMEM((columns, freq, columns), jnp.float32),
            dma((columns,)), dma,
        ],
        compiler_params=pltpu.CompilerParams(vmem_limit_bytes=16 * 1024 * 1024),
    )(values, gram)
    return jnp.transpose(modes, (2, 0, 1, 3)), jnp.transpose(factor, (1, 0, 2))


def on_device(snapshots, weights, bins):
    seg_count = lax.axis_size("seg")
    var_count = lax.axis_size("var")
    space_count = lax.axis_size("space")
    frames, variables, cell_dev = snapshots.shape
    flat_rows = variables * cell_dev
    hop_len = frames // 2
    block_count = 2 * seg_count - 1
    freq_dev = bins.shape[0] // (seg_count * var_count)
    own = snapshots.reshape(frames, flat_rows)
    start_bin = (lax.axis_index("seg") * var_count + lax.axis_index("var")) * freq_dev
    chosen = lax.dynamic_slice_in_dim(bins, start_bin, freq_dev)
    piece = lax.all_gather(own, "seg", axis=0, tiled=True)
    count = piece.shape[0]
    moments = jnp.arange(count, dtype=jnp.int32)
    offset = moments[:, None] - hop_len * jnp.arange(block_count, dtype=jnp.int32)[None, :]
    inside = (offset >= 0) & (offset < frames)
    safe_offset = jnp.where(inside, offset, 0)
    cosine, sine = window_basis(safe_offset[:, :, None], chosen[None, None, :], frames)
    coeffs = jnp.stack([cosine, sine], 3) * inside[:, :, None, None].astype(jnp.float32)
    coeffs = jnp.transpose(coeffs, (0, 2, 3, 1)).reshape(count, freq_dev * 2 * block_count)
    coeffs = coeffs.astype(jnp.bfloat16)
    summed = jnp.einsum("pk,pr->kr", coeffs, piece, preferred_element_type=jnp.float32)
    spectra = summed.astype(jnp.bfloat16).reshape(freq_dev, 2 * block_count, flat_rows)
    values = spectra.astype(jnp.float32)
    scaled = values * weights.reshape(flat_rows)
    local_gram = jnp.einsum("fir,fjr->fij", scaled, values, precision=lax.Precision.HIGHEST)
    local_gram = local_gram / (variables * cell_dev * space_count)
    lower = jnp.linalg.cholesky(lax.psum(local_gram, "space"))
    inverse = invert_lower(lower)
    modes = jnp.einsum("fij,fjr->fir", inverse, values, precision=lax.Precision.HIGHEST)
    modes = modes.reshape(freq_dev, 2 * block_count, variables, cell_dev)
    return (modes, jnp.swapaxes(lower, 1, 2))


def per_device(snapshots, weights, bins):
    seg_count = lax.axis_size("seg")
    frames, variables, cells = snapshots.shape
    freq_dev = bins.shape[0] // (seg_count * lax.axis_size("var"))
    fits = seg_count == 2 and lax.axis_size("var") == 2 and freq_dev == 8 and cells % 128 == 0
    fits = fits and frames >= 256 and frames & (frames - 1) == 0 and lax.axis_size("space") > 1
    return (on_device_kernel if fits else on_device)(snapshots, weights, bins)


def solution(mesh):
    return jax.shard_map(
        per_device,
        mesh=mesh,
        in_specs=(P(("grp", "seg"), None, "space"), P(None, ("grp", "space")), P()),
        out_specs=(
            P(("seg", "var"), None, None, ("grp", "space")),
            P(("grp", "seg", "var"), None, None),
        ),
        check_vma=False,
    )
```

```python
import functools
import math

import jax
import jax.numpy as jnp
from jax import lax
from jax.experimental import pallas as pl
from jax.experimental.pallas import tpu as pltpu
from jax.sharding import PartitionSpec as P


def window_basis(offset, bin_index, length):
    phase = offset * bin_index % length
    angle = 2.0 * math.pi / length * phase.astype(jnp.float32)
    taper = 0.5 - 0.5 * jnp.cos(2.0 * math.pi / length * offset.astype(jnp.float32))
    factor = taper / math.sqrt(0.375 * length)
    return (factor * jnp.cos(angle), -factor * jnp.sin(angle))


def invert_lower(lower):
    identity = jnp.eye(lower.shape[-1], dtype=lower.dtype)

    def solve_single(single):
        return jax.scipy.linalg.solve_triangular(single, identity, lower=True)

    return jax.vmap(solve_single)(lower)


MESH = pl.DeviceIdType.MESH


def cosine_of(phase, length):
    quarter = jnp.abs(phase - length // 2) - length // 4
    x = quarter.astype(jnp.float32) * (2.0 * math.pi / length)
    y = x * x
    poly = -1.0 / 39916800.0
    for term in (1.0 / 362880.0, -1.0 / 5040.0, 1.0 / 120.0, -1.0 / 6.0, 1.0):
        poly = poly * y + term
    return x * poly


def basis_rows(bins_ref, frames, seg, var, var_count):
    freq = 8
    shape = (freq, frames)
    frame = lax.broadcasted_iota(jnp.int32, shape, 1)
    row = lax.broadcasted_iota(jnp.int32, shape, 0)
    half = frames // 2
    taper = (0.5 - 0.5 * cosine_of(frame, frames)) / math.sqrt(0.375 * frames)
    second = (lax.broadcasted_iota(jnp.int32, (2 * freq, frames), 1) >= half).astype(jnp.int32)
    overlap = second == 1 - seg
    rows = []
    for group in range(2):
        owner = 1 - seg if group == 0 else seg
        first = (owner * var_count + var) * freq
        bin_of = jnp.zeros(shape, jnp.int32)
        for f in range(freq):
            bin_of = jnp.where(row == f, bins_ref[first + f], bin_of)
        phase = (frame * bin_of) & (frames - 1)
        cosine = taper * cosine_of(phase, frames)
        sine = taper * cosine_of((phase + frames // 4) & (frames - 1), frames)
        whole = jnp.concatenate([cosine, sine], 0)
        shared = jnp.concatenate([whole[:, half:], whole[:, :half]], 1)
        rows += [whole, jnp.where(overlap, shared, 0.0)]
    return jnp.concatenate(rows, 0).astype(jnp.bfloat16)


def kernel(space_count, var_count, x_hbm, w_hbm, bins_hbm, values, gram_ref,
           x_vmem, w_ref, bins_ref, own_half, send, recv, gram_buf,
           x_sem, w_sem, bins_sem, send_sem, recv_sem, g_send_sem, g_recv_sem):
    variables, frames, cells = x_hbm.shape
    freq = 8
    rows = 2 * freq
    seg = lax.axis_index("seg")
    var = lax.axis_index("var")
    me = lax.axis_index("space")
    other = 1 - seg
    bins_load = pltpu.make_async_copy(bins_hbm, bins_ref, bins_sem)
    bins_load.start()
    loads = []
    for v in range(variables):
        load = pltpu.make_async_copy(x_hbm.at[v], x_vmem.at[v], x_sem.at[v])
        load.start()
        loads.append(load)

    w_load = pltpu.make_async_copy(w_hbm, w_ref, w_sem)
    w_load.start()

    barrier = pltpu.get_barrier_semaphore()
    pl.semaphore_signal(barrier, inc=1, device_id={"seg": other}, device_id_type=MESH)
    for d in range(1, space_count):
        pl.semaphore_signal(
            barrier, inc=1, device_id={"space": lax.rem(me + d, space_count)}, device_id_type=MESH)

    bins_load.wait()
    basis = basis_rows(bins_ref, frames, seg, var, var_count)

    copies = []
    for v in range(variables):
        loads[v].wait()
        summed = jnp.dot(basis[:2 * rows], x_vmem[v], preferred_element_type=jnp.float32)
        send[v] = summed.astype(send.dtype)
        if v == 0:
            pl.semaphore_wait(barrier, space_count)
        copy = pltpu.make_async_remote_copy(
            src_ref=send.at[v], dst_ref=recv.at[v], send_sem=send_sem.at[v], recv_sem=recv_sem.at[v],
            device_id={"seg": other}, device_id_type=MESH)
        pl.when(var == 0)(copy.start)
        copies.append(copy)
    for v in range(variables):
        summed = jnp.dot(basis[2 * rows:], x_vmem[v], preferred_element_type=jnp.float32)
        own = summed[:rows].astype(jnp.bfloat16).astype(jnp.float32)
        own_half[v] = summed[rows:]
        for part in range(2):
            values[3 * part + 2 * seg, v] = own[part * freq:(part + 1) * freq]
    for copy in copies:
        pl.when(var != 0)(copy.start)

    w_load.wait()
    columns = 6
    pairs = [(i, j) for i in range(columns) for j in range(i + 1)]
    sums = [None] * len(pairs)
    for v in range(variables):
        copies[v].wait_recv()
        far = recv[v].astype(jnp.float32)
        total = own_half[v] + far[rows:]
        total = total.astype(jnp.bfloat16).astype(jnp.float32)
        for part in range(2):
            values[3 * part + 1, v] = total[part * freq:(part + 1) * freq]
            values[3 * part + 2 * other, v] = far[part * freq:(part + 1) * freq]
        for at in range(0, cells, 128):
            one = pl.ds(at, 128)
            weight = jnp.broadcast_to(w_ref[v:v + 1, one], (freq, 128))
            plain = [values[i, v, :, one] for i in range(columns)]
            scaled = [p * weight for p in plain]
            for n, (i, j) in enumerate(pairs):
                term = scaled[i] * plain[j]
                sums[n] = term if sums[n] is None else sums[n] + term

    lane = lax.broadcasted_iota(jnp.int32, (freq, 128), 1)
    packed = jnp.zeros((freq, 128), jnp.float32)
    for n in range(len(pairs)):
        packed = jnp.where(lane == n, jnp.sum(sums[n], axis=1, keepdims=True), packed)
    gram_buf[me] = packed
    g_copies = []
    for d in range(1, space_count):
        copy = pltpu.make_async_remote_copy(
            src_ref=gram_buf.at[me], dst_ref=gram_buf.at[me],
            send_sem=g_send_sem.at[d - 1], recv_sem=g_recv_sem.at[d - 1],
            device_id={"space": lax.rem(me + d, space_count)}, device_id_type=MESH)
        copy.start()
        g_copies.append(copy)
    for copy in g_copies:
        copy.wait_recv()
    gram = gram_buf[0]
    for d in range(1, space_count):
        gram = gram + gram_buf[d]
    gram_ref[...] = gram

    for copy in copies + g_copies:
        copy.wait_send()


def modes_kernel(space_count, values, gram_ref, modes_hbm, factor_hbm, modes_vmem, factor_ref, modes_sem, factor_sem):
    columns, variables, freq, cells = values.shape
    pairs = [(i, j) for i in range(columns) for j in range(i + 1)]
    lane = lax.broadcasted_iota(jnp.int32, (freq, 128), 1)
    gram = gram_ref[...] * (1.0 / (variables * cells * space_count))
    entry = {
        pair: jnp.broadcast_to(gram[:, n:n + 1], (freq, 128)) for n, pair in enumerate(pairs)}

    lower, inverse = {}, {}
    for j in range(columns):
        rest = entry[j, j]
        for k in range(j):
            rest = rest - lower[j, k] * lower[j, k]
        inverse[j, j] = lax.rsqrt(rest)
        lower[j, j] = rest * inverse[j, j]
        for i in range(j + 1, columns):
            rest = entry[i, j]
            for k in range(j):
                rest = rest - lower[i, k] * lower[j, k]
            lower[i, j] = rest * inverse[j, j]
    for j in range(columns):
        for i in range(j + 1, columns):
            total = lower[i, j] * inverse[j, j]
            for k in range(j + 1, i):
                total = total + lower[i, k] * inverse[k, j]
            inverse[i, j] = -total * inverse[i, i]

    for i in range(columns):
        line = jnp.zeros((freq, 128), jnp.float32)
        for j in range(i, columns):
            line = jnp.where(lane == j, lower[j, i], line)
        factor_ref[i] = line[:, :columns]

    copies = [pltpu.make_async_copy(factor_ref, factor_hbm, factor_sem)]
    copies[0].start()
    for i in range(columns):
        for v in range(variables):
            for at in range(0, cells, 128):
                one = pl.ds(at, 128)
                mode = inverse[i, 0] * values[0, v, :, one]
                for j in range(1, i + 1):
                    mode = mode + inverse[i, j] * values[j, v, :, one]
                modes_vmem[i, v, :, one] = mode
        copy = pltpu.make_async_copy(modes_vmem.at[i], modes_hbm.at[i], modes_sem.at[i])
        copy.start()
        copies.append(copy)
    for copy in copies:
        copy.wait()


def on_device_kernel(snapshots, weights, bins):
    frames, variables, cells = snapshots.shape
    space_count = lax.axis_size("space")
    freq, columns = 8, 6
    rows = 2 * freq
    dma = pltpu.SemaphoreType.DMA
    inputs = [jnp.transpose(snapshots, (1, 0, 2)), weights, bins]
    inputs = [pltpu.with_memory_space_constraint(value, pltpu.HBM) for value in inputs]
    values, gram = pl.pallas_call(
        functools.partial(kernel, space_count, lax.axis_size("var")),
        out_shape=(
            jax.ShapeDtypeStruct((columns, variables, freq, cells), jnp.float32),
            jax.ShapeDtypeStruct((freq, 128), jnp.float32),
        ),
        in_specs=[
            pl.BlockSpec(memory_space=pltpu.HBM),
            pl.BlockSpec(memory_space=pltpu.HBM),
            pl.BlockSpec(memory_space=pltpu.HBM),
        ],
        out_specs=(pl.BlockSpec(memory_space=pltpu.VMEM),) * 2,
        scratch_shapes=[
            pltpu.VMEM((variables, frames, cells), jnp.bfloat16),
            pltpu.VMEM((variables, cells), jnp.float32),
            pltpu.SMEM(bins.shape, jnp.int32),
            pltpu.VMEM((variables, rows, cells), jnp.float32),
            pltpu.VMEM((variables, 2 * rows, cells), jnp.bfloat16),
            pltpu.VMEM((variables, 2 * rows, cells), jnp.bfloat16),
            pltpu.VMEM((space_count, freq, 128), jnp.float32),
            dma((variables,)), dma, dma,
            dma((variables,)), dma((variables,)),
            dma((space_count - 1,)), dma((space_count - 1,)),
        ],
        compiler_params=pltpu.CompilerParams(
            collective_id=0, has_side_effects=True, vmem_limit_bytes=32 * 1024 * 1024),
    )(*inputs)
    modes, factor = pl.pallas_call(
        functools.partial(modes_kernel, space_count),
        out_shape=(
            jax.ShapeDtypeStruct((columns, variables, freq, cells), jnp.float32),
            jax.ShapeDtypeStruct((columns, freq, columns), jnp.float32),
        ),
        in_specs=[pl.BlockSpec(memory_space=pltpu.VMEM)] * 2,
        out_specs=(pl.BlockSpec(memory_space=pltpu.HBM),) * 2,
        scratch_shapes=[
            pltpu.VMEM((columns, variables, freq, cells), jnp.float32),
            pltpu.VMEM((columns, freq, columns), jnp.float32),
            dma((columns,)), dma,
        ],
        compiler_params=pltpu.CompilerParams(vmem_limit_bytes=16 * 1024 * 1024),
    )(values, gram)
    return jnp.transpose(modes, (2, 0, 1, 3)), jnp.transpose(factor, (1, 0, 2))


def on_device(snapshots, weights, bins):
    seg_count = lax.axis_size("seg")
    var_count = lax.axis_size("var")
    space_count = lax.axis_size("space")
    frames, variables, cell_dev = snapshots.shape
    flat_rows = variables * cell_dev
    hop_len = frames // 2
    block_count = 2 * seg_count - 1
    freq_dev = bins.shape[0] // (seg_count * var_count)
    own = snapshots.reshape(frames, flat_rows)
    start_bin = (lax.axis_index("seg") * var_count + lax.axis_index("var")) * freq_dev
    chosen = lax.dynamic_slice_in_dim(bins, start_bin, freq_dev)
    piece = lax.all_gather(own, "seg", axis=0, tiled=True)
    count = piece.shape[0]
    moments = jnp.arange(count, dtype=jnp.int32)
    offset = moments[:, None] - hop_len * jnp.arange(block_count, dtype=jnp.int32)[None, :]
    inside = (offset >= 0) & (offset < frames)
    safe_offset = jnp.where(inside, offset, 0)
    cosine, sine = window_basis(safe_offset[:, :, None], chosen[None, None, :], frames)
    coeffs = jnp.stack([cosine, sine], 3) * inside[:, :, None, None].astype(jnp.float32)
    coeffs = jnp.transpose(coeffs, (0, 2, 3, 1)).reshape(count, freq_dev * 2 * block_count)
    coeffs = coeffs.astype(jnp.bfloat16)
    summed = jnp.einsum("pk,pr->kr", coeffs, piece, preferred_element_type=jnp.float32)
    spectra = summed.astype(jnp.bfloat16).reshape(freq_dev, 2 * block_count, flat_rows)
    values = spectra.astype(jnp.float32)
    scaled = values * weights.reshape(flat_rows)
    local_gram = jnp.einsum("fir,fjr->fij", scaled, values, precision=lax.Precision.HIGHEST)
    local_gram = local_gram / (variables * cell_dev * space_count)
    lower = jnp.linalg.cholesky(lax.psum(local_gram, "space"))
    inverse = invert_lower(lower)
    modes = jnp.einsum("fij,fjr->fir", inverse, values, precision=lax.Precision.HIGHEST)
    modes = modes.reshape(freq_dev, 2 * block_count, variables, cell_dev)
    return (modes, jnp.swapaxes(lower, 1, 2))


def per_device(snapshots, weights, bins):
    seg_count = lax.axis_size("seg")
    frames, variables, cells = snapshots.shape
    freq_dev = bins.shape[0] // (seg_count * lax.axis_size("var"))
    fits = seg_count == 2 and lax.axis_size("var") == 2 and freq_dev == 8 and cells % 128 == 0
    fits = fits and frames >= 256 and frames & (frames - 1) == 0 and lax.axis_size("space") > 1
    return (on_device_kernel if fits else on_device)(snapshots, weights, bins)


def solution(mesh):
    return jax.shard_map(
        per_device,
        mesh=mesh,
        in_specs=(P(("grp", "seg"), None, "space"), P(None, ("grp", "space")), P()),
        out_specs=(
            P(("seg", "var"), None, None, ("grp", "space")),
            P(("grp", "seg", "var"), None, None),
        ),
        check_vma=False,
    )
```

```python
import functools
import math

import jax
import jax.numpy as jnp
from jax import lax
from jax.experimental import pallas as pl
from jax.experimental.pallas import tpu as pltpu
from jax.sharding import PartitionSpec as P


def window_basis(offset, bin_index, length):
    phase = offset * bin_index % length
    angle = 2.0 * math.pi / length * phase.astype(jnp.float32)
    taper = 0.5 - 0.5 * jnp.cos(2.0 * math.pi / length * offset.astype(jnp.float32))
    factor = taper / math.sqrt(0.375 * length)
    return (factor * jnp.cos(angle), -factor * jnp.sin(angle))


def invert_lower(lower):
    identity = jnp.eye(lower.shape[-1], dtype=lower.dtype)

    def solve_single(single):
        return jax.scipy.linalg.solve_triangular(single, identity, lower=True)

    return jax.vmap(solve_single)(lower)


MESH = pl.DeviceIdType.MESH


def cosine_of(phase, length):
    quarter = jnp.abs(phase - length // 2) - length // 4
    x = quarter.astype(jnp.float32) * (2.0 * math.pi / length)
    y = x * x
    poly = -1.0 / 39916800.0
    for term in (1.0 / 362880.0, -1.0 / 5040.0, 1.0 / 120.0, -1.0 / 6.0, 1.0):
        poly = poly * y + term
    return x * poly


def basis_rows(bins_ref, frames, seg, var, var_count):
    freq = 8
    shape = (freq, frames)
    frame = lax.broadcasted_iota(jnp.int32, shape, 1)
    row = lax.broadcasted_iota(jnp.int32, shape, 0)
    half = frames // 2
    taper = (0.5 - 0.5 * cosine_of(frame, frames)) / math.sqrt(0.375 * frames)
    second = (lax.broadcasted_iota(jnp.int32, (2 * freq, frames), 1) >= half).astype(jnp.int32)
    overlap = second == 1 - seg
    rows = []
    for group in range(2):
        owner = 1 - seg if group == 0 else seg
        first = (owner * var_count + var) * freq
        bin_of = jnp.zeros(shape, jnp.int32)
        for f in range(freq):
            bin_of = jnp.where(row == f, bins_ref[first + f], bin_of)
        phase = (frame * bin_of) & (frames - 1)
        cosine = taper * cosine_of(phase, frames)
        sine = taper * cosine_of((phase + frames // 4) & (frames - 1), frames)
        whole = jnp.concatenate([cosine, sine], 0)
        shared = jnp.concatenate([whole[:, half:], whole[:, :half]], 1)
        rows += [whole, jnp.where(overlap, shared, 0.0)]
    return jnp.concatenate(rows, 0).astype(jnp.bfloat16)


def kernel(space_count, var_count, x_hbm, w_hbm, bins_hbm, values, gram_ref,
           x_vmem, w_ref, bins_ref, own_half, send, recv, gram_buf,
           x_sem, w_sem, bins_sem, send_sem, recv_sem, g_send_sem, g_recv_sem):
    variables, frames, cells = x_hbm.shape
    freq = 8
    rows = 2 * freq
    seg = lax.axis_index("seg")
    var = lax.axis_index("var")
    me = lax.axis_index("space")
    other = 1 - seg
    bins_load = pltpu.make_async_copy(bins_hbm, bins_ref, bins_sem)
    bins_load.start()
    loads = []
    for v in range(variables):
        load = pltpu.make_async_copy(x_hbm.at[v], x_vmem.at[v], x_sem.at[v])
        load.start()
        loads.append(load)

    w_load = pltpu.make_async_copy(w_hbm, w_ref, w_sem)
    w_load.start()

    barrier = pltpu.get_barrier_semaphore()
    pl.semaphore_signal(barrier, inc=1, device_id={"seg": other}, device_id_type=MESH)
    for d in range(1, space_count):
        pl.semaphore_signal(
            barrier, inc=1, device_id={"space": lax.rem(me + d, space_count)}, device_id_type=MESH)

    bins_load.wait()
    basis = basis_rows(bins_ref, frames, seg, var, var_count)

    copies = []
    for v in range(variables):
        loads[v].wait()
        summed = jnp.dot(basis, x_vmem[v], preferred_element_type=jnp.float32)
        send[v] = summed[:2 * rows].astype(send.dtype)
        if v == 0:
            pl.semaphore_wait(barrier, space_count)
        copy = pltpu.make_async_remote_copy(
            src_ref=send.at[v], dst_ref=recv.at[v], send_sem=send_sem.at[v], recv_sem=recv_sem.at[v],
            device_id={"seg": other}, device_id_type=MESH)
        pl.when(var == 0)(copy.start)
        copies.append(copy)
        own = summed[2 * rows:3 * rows].astype(jnp.bfloat16).astype(jnp.float32)
        own_half[v] = summed[3 * rows:]
        for part in range(2):
            values[3 * part + 2 * seg, v] = own[part * freq:(part + 1) * freq]

    @pl.when(var != 0)
    def _():
        for copy in copies:
            copy.start()

    w_load.wait()
    columns = 6
    pairs = [(i, j) for i in range(columns) for j in range(i + 1)]
    sums = [None] * len(pairs)
    for v in range(variables):
        copies[v].wait_recv()
        far = recv[v].astype(jnp.float32)
        total = own_half[v] + far[rows:]
        total = total.astype(jnp.bfloat16).astype(jnp.float32)
        for part in range(2):
            values[3 * part + 1, v] = total[part * freq:(part + 1) * freq]
            values[3 * part + 2 * other, v] = far[part * freq:(part + 1) * freq]
        for at in range(0, cells, 128):
            one = pl.ds(at, 128)
            weight = jnp.broadcast_to(w_ref[v:v + 1, one], (freq, 128))
            plain = [values[i, v, :, one] for i in range(columns)]
            scaled = [p * weight for p in plain]
            for n, (i, j) in enumerate(pairs):
                term = scaled[i] * plain[j]
                sums[n] = term if sums[n] is None else sums[n] + term

    lane = lax.broadcasted_iota(jnp.int32, (freq, 128), 1)
    packed = jnp.zeros((freq, 128), jnp.float32)
    for n in range(len(pairs)):
        packed = jnp.where(lane == n, jnp.sum(sums[n], axis=1, keepdims=True), packed)
    gram_buf[me] = packed
    g_copies = []
    for d in range(1, space_count):
        copy = pltpu.make_async_remote_copy(
            src_ref=gram_buf.at[me], dst_ref=gram_buf.at[me],
            send_sem=g_send_sem.at[d - 1], recv_sem=g_recv_sem.at[d - 1],
            device_id={"space": lax.rem(me + d, space_count)}, device_id_type=MESH)
        copy.start()
        g_copies.append(copy)
    for copy in g_copies:
        copy.wait_recv()
    gram = gram_buf[0]
    for d in range(1, space_count):
        gram = gram + gram_buf[d]
    gram_ref[...] = gram

    for copy in copies + g_copies:
        copy.wait_send()


def modes_kernel(space_count, values, gram_ref, modes_hbm, factor_hbm, modes_vmem, factor_ref, modes_sem, factor_sem):
    columns, variables, freq, cells = values.shape
    pairs = [(i, j) for i in range(columns) for j in range(i + 1)]
    lane = lax.broadcasted_iota(jnp.int32, (freq, 128), 1)
    gram = gram_ref[...] * (1.0 / (variables * cells * space_count))
    entry = {
        pair: jnp.broadcast_to(gram[:, n:n + 1], (freq, 128)) for n, pair in enumerate(pairs)}

    lower, inverse = {}, {}
    for j in range(columns):
        rest = entry[j, j]
        for k in range(j):
            rest = rest - lower[j, k] * lower[j, k]
        inverse[j, j] = lax.rsqrt(rest)
        lower[j, j] = rest * inverse[j, j]
        for i in range(j + 1, columns):
            rest = entry[i, j]
            for k in range(j):
                rest = rest - lower[i, k] * lower[j, k]
            lower[i, j] = rest * inverse[j, j]
    for j in range(columns):
        for i in range(j + 1, columns):
            total = lower[i, j] * inverse[j, j]
            for k in range(j + 1, i):
                total = total + lower[i, k] * inverse[k, j]
            inverse[i, j] = -total * inverse[i, i]

    for i in range(columns):
        line = jnp.zeros((freq, 128), jnp.float32)
        for j in range(i, columns):
            line = jnp.where(lane == j, lower[j, i], line)
        factor_ref[i] = line[:, :columns]

    copies = [pltpu.make_async_copy(factor_ref, factor_hbm, factor_sem)]
    copies[0].start()
    for i in range(columns):
        for v in range(variables):
            for at in range(0, cells, 128):
                one = pl.ds(at, 128)
                mode = inverse[i, 0] * values[0, v, :, one]
                for j in range(1, i + 1):
                    mode = mode + inverse[i, j] * values[j, v, :, one]
                modes_vmem[i, v, :, one] = mode
        copy = pltpu.make_async_copy(modes_vmem.at[i], modes_hbm.at[i], modes_sem.at[i])
        copy.start()
        copies.append(copy)
    for copy in copies:
        copy.wait()


def on_device_kernel(snapshots, weights, bins):
    frames, variables, cells = snapshots.shape
    space_count = lax.axis_size("space")
    freq, columns = 8, 6
    rows = 2 * freq
    dma = pltpu.SemaphoreType.DMA
    inputs = [jnp.transpose(snapshots, (1, 0, 2)), weights, bins]
    inputs = [pltpu.with_memory_space_constraint(value, pltpu.HBM) for value in inputs]
    values, gram = pl.pallas_call(
        functools.partial(kernel, space_count, lax.axis_size("var")),
        out_shape=(
            jax.ShapeDtypeStruct((columns, variables, freq, cells), jnp.float32),
            jax.ShapeDtypeStruct((freq, 128), jnp.float32),
        ),
        in_specs=[
            pl.BlockSpec(memory_space=pltpu.HBM),
            pl.BlockSpec(memory_space=pltpu.HBM),
            pl.BlockSpec(memory_space=pltpu.HBM),
        ],
        out_specs=(pl.BlockSpec(memory_space=pltpu.VMEM),) * 2,
        scratch_shapes=[
            pltpu.VMEM((variables, frames, cells), jnp.bfloat16),
            pltpu.VMEM((variables, cells), jnp.float32),
            pltpu.SMEM(bins.shape, jnp.int32),
            pltpu.VMEM((variables, rows, cells), jnp.float32),
            pltpu.VMEM((variables, 2 * rows, cells), jnp.bfloat16),
            pltpu.VMEM((variables, 2 * rows, cells), jnp.bfloat16),
            pltpu.VMEM((space_count, freq, 128), jnp.float32),
            dma((variables,)), dma, dma,
            dma((variables,)), dma((variables,)),
            dma((space_count - 1,)), dma((space_count - 1,)),
        ],
        compiler_params=pltpu.CompilerParams(
            collective_id=0, has_side_effects=True, vmem_limit_bytes=32 * 1024 * 1024),
    )(*inputs)
    modes, factor = pl.pallas_call(
        functools.partial(modes_kernel, space_count),
        out_shape=(
            jax.ShapeDtypeStruct((columns, variables, freq, cells), jnp.float32),
            jax.ShapeDtypeStruct((columns, freq, columns), jnp.float32),
        ),
        in_specs=[pl.BlockSpec(memory_space=pltpu.VMEM)] * 2,
        out_specs=(pl.BlockSpec(memory_space=pltpu.HBM),) * 2,
        scratch_shapes=[
            pltpu.VMEM((columns, variables, freq, cells), jnp.float32),
            pltpu.VMEM((columns, freq, columns), jnp.float32),
            dma((columns,)), dma,
        ],
        compiler_params=pltpu.CompilerParams(vmem_limit_bytes=16 * 1024 * 1024),
    )(values, gram)
    return jnp.transpose(modes, (2, 0, 1, 3)), jnp.transpose(factor, (1, 0, 2))


def on_device(snapshots, weights, bins):
    seg_count = lax.axis_size("seg")
    var_count = lax.axis_size("var")
    space_count = lax.axis_size("space")
    frames, variables, cell_dev = snapshots.shape
    flat_rows = variables * cell_dev
    hop_len = frames // 2
    block_count = 2 * seg_count - 1
    freq_dev = bins.shape[0] // (seg_count * var_count)
    own = snapshots.reshape(frames, flat_rows)
    start_bin = (lax.axis_index("seg") * var_count + lax.axis_index("var")) * freq_dev
    chosen = lax.dynamic_slice_in_dim(bins, start_bin, freq_dev)
    piece = lax.all_gather(own, "seg", axis=0, tiled=True)
    count = piece.shape[0]
    moments = jnp.arange(count, dtype=jnp.int32)
    offset = moments[:, None] - hop_len * jnp.arange(block_count, dtype=jnp.int32)[None, :]
    inside = (offset >= 0) & (offset < frames)
    safe_offset = jnp.where(inside, offset, 0)
    cosine, sine = window_basis(safe_offset[:, :, None], chosen[None, None, :], frames)
    coeffs = jnp.stack([cosine, sine], 3) * inside[:, :, None, None].astype(jnp.float32)
    coeffs = jnp.transpose(coeffs, (0, 2, 3, 1)).reshape(count, freq_dev * 2 * block_count)
    coeffs = coeffs.astype(jnp.bfloat16)
    summed = jnp.einsum("pk,pr->kr", coeffs, piece, preferred_element_type=jnp.float32)
    spectra = summed.astype(jnp.bfloat16).reshape(freq_dev, 2 * block_count, flat_rows)
    values = spectra.astype(jnp.float32)
    scaled = values * weights.reshape(flat_rows)
    local_gram = jnp.einsum("fir,fjr->fij", scaled, values, precision=lax.Precision.HIGHEST)
    local_gram = local_gram / (variables * cell_dev * space_count)
    lower = jnp.linalg.cholesky(lax.psum(local_gram, "space"))
    inverse = invert_lower(lower)
    modes = jnp.einsum("fij,fjr->fir", inverse, values, precision=lax.Precision.HIGHEST)
    modes = modes.reshape(freq_dev, 2 * block_count, variables, cell_dev)
    return (modes, jnp.swapaxes(lower, 1, 2))


def per_device(snapshots, weights, bins):
    seg_count = lax.axis_size("seg")
    frames, variables, cells = snapshots.shape
    freq_dev = bins.shape[0] // (seg_count * lax.axis_size("var"))
    fits = seg_count == 2 and lax.axis_size("var") == 2 and freq_dev == 8 and cells % 128 == 0
    fits = fits and frames >= 256 and frames & (frames - 1) == 0 and lax.axis_size("space") > 1
    return (on_device_kernel if fits else on_device)(snapshots, weights, bins)


def solution(mesh):
    return jax.shard_map(
        per_device,
        mesh=mesh,
        in_specs=(P(("grp", "seg"), None, "space"), P(None, ("grp", "space")), P()),
        out_specs=(
            P(("seg", "var"), None, None, ("grp", "space")),
            P(("grp", "seg", "var"), None, None),
        ),
        check_vma=False,
    )
```

```python
import functools
import math

import jax
import jax.numpy as jnp
from jax import lax
from jax.experimental import pallas as pl
from jax.experimental.pallas import tpu as pltpu
from jax.sharding import PartitionSpec as P


def window_basis(offset, bin_index, length):
    phase = offset * bin_index % length
    angle = 2.0 * math.pi / length * phase.astype(jnp.float32)
    taper = 0.5 - 0.5 * jnp.cos(2.0 * math.pi / length * offset.astype(jnp.float32))
    factor = taper / math.sqrt(0.375 * length)
    return (factor * jnp.cos(angle), -factor * jnp.sin(angle))


def invert_lower(lower):
    identity = jnp.eye(lower.shape[-1], dtype=lower.dtype)

    def solve_single(single):
        return jax.scipy.linalg.solve_triangular(single, identity, lower=True)

    return jax.vmap(solve_single)(lower)


MESH = pl.DeviceIdType.MESH


def cosine_of(phase, length):
    quarter = jnp.abs(phase - length // 2) - length // 4
    x = quarter.astype(jnp.float32) * (2.0 * math.pi / length)
    y = x * x
    poly = -1.0 / 39916800.0
    for term in (1.0 / 362880.0, -1.0 / 5040.0, 1.0 / 120.0, -1.0 / 6.0, 1.0):
        poly = poly * y + term
    return x * poly


def basis_rows(bins_ref, frames, seg, var, var_count):
    freq = 8
    shape = (freq, frames)
    frame = lax.broadcasted_iota(jnp.int32, shape, 1)
    row = lax.broadcasted_iota(jnp.int32, shape, 0)
    half = frames // 2
    taper = (0.5 - 0.5 * cosine_of(frame, frames)) / math.sqrt(0.375 * frames)
    second = (lax.broadcasted_iota(jnp.int32, (2 * freq, frames), 1) >= half).astype(jnp.int32)
    overlap = second == 1 - seg
    rows = []
    for group in range(2):
        owner = 1 - seg if group == 0 else seg
        first = (owner * var_count + var) * freq
        bin_of = jnp.zeros(shape, jnp.int32)
        for f in range(freq):
            bin_of = jnp.where(row == f, bins_ref[first + f], bin_of)
        phase = (frame * bin_of) & (frames - 1)
        cosine = taper * cosine_of(phase, frames)
        sine = taper * cosine_of((phase + frames // 4) & (frames - 1), frames)
        whole = jnp.concatenate([cosine, sine], 0)
        shared = jnp.concatenate([whole[:, half:], whole[:, :half]], 1)
        rows += [whole, jnp.where(overlap, shared, 0.0)]
    return jnp.concatenate(rows, 0).astype(jnp.bfloat16)


def kernel(space_count, var_count, x_hbm, w_hbm, bins_hbm, values, gram_ref,
           x_vmem, w_ref, bins_ref, own_half, send, recv, gram_buf,
           x_sem, w_sem, bins_sem, send_sem, recv_sem, g_send_sem, g_recv_sem):
    variables, frames, cells = x_hbm.shape
    freq = 8
    rows = 2 * freq
    seg = lax.axis_index("seg")
    var = lax.axis_index("var")
    me = lax.axis_index("space")
    other = 1 - seg
    bins_load = pltpu.make_async_copy(bins_hbm, bins_ref, bins_sem)
    bins_load.start()
    loads = []
    for v in range(variables):
        load = pltpu.make_async_copy(x_hbm.at[v], x_vmem.at[v], x_sem.at[v])
        load.start()
        loads.append(load)

    w_load = pltpu.make_async_copy(w_hbm, w_ref, w_sem)
    w_load.start()

    barrier = pltpu.get_barrier_semaphore()
    pl.semaphore_signal(barrier, inc=1, device_id={"seg": other}, device_id_type=MESH)
    for d in range(1, space_count):
        pl.semaphore_signal(
            barrier, inc=1, device_id={"space": lax.rem(me + d, space_count)}, device_id_type=MESH)

    bins_load.wait()
    basis = basis_rows(bins_ref, frames, seg, var, var_count)

    pl.semaphore_wait(barrier, space_count)
    copies = [
        pltpu.make_async_remote_copy(
            src_ref=send.at[v], dst_ref=recv.at[v], send_sem=send_sem.at[v], recv_sem=recv_sem.at[v],
            device_id={"seg": other}, device_id_type=MESH)
        for v in range(variables)]

    def transform(v):
        loads[v].wait()
        summed = jnp.dot(basis, x_vmem[v], preferred_element_type=jnp.float32)
        send[v] = summed[:2 * rows].astype(send.dtype)
        own = summed[2 * rows:3 * rows].astype(jnp.bfloat16).astype(jnp.float32)
        own_half[v] = summed[3 * rows:]
        for part in range(2):
            values[3 * part + 2 * seg, v] = own[part * freq:(part + 1) * freq]

    @pl.when(var == 0)
    def _():
        for v in range(variables):
            transform(v)
            copies[v].start()

    @pl.when(var != 0)
    def _():
        for v in range(variables):
            transform(v)
        for copy in copies:
            copy.start()

    w_load.wait()
    columns = 6
    pairs = [(i, j) for i in range(columns) for j in range(i + 1)]
    sums = [None] * len(pairs)
    for v in range(variables):
        copies[v].wait_recv()
        far = recv[v].astype(jnp.float32)
        total = own_half[v] + far[rows:]
        total = total.astype(jnp.bfloat16).astype(jnp.float32)
        for part in range(2):
            values[3 * part + 1, v] = total[part * freq:(part + 1) * freq]
            values[3 * part + 2 * other, v] = far[part * freq:(part + 1) * freq]
        for at in range(0, cells, 128):
            one = pl.ds(at, 128)
            weight = jnp.broadcast_to(w_ref[v:v + 1, one], (freq, 128))
            plain = [values[i, v, :, one] for i in range(columns)]
            scaled = [p * weight for p in plain]
            for n, (i, j) in enumerate(pairs):
                term = scaled[i] * plain[j]
                sums[n] = term if sums[n] is None else sums[n] + term

    lane = lax.broadcasted_iota(jnp.int32, (freq, 128), 1)
    packed = jnp.zeros((freq, 128), jnp.float32)
    for n in range(len(pairs)):
        packed = jnp.where(lane == n, jnp.sum(sums[n], axis=1, keepdims=True), packed)
    gram_buf[me] = packed
    g_copies = []
    for d in range(1, space_count):
        copy = pltpu.make_async_remote_copy(
            src_ref=gram_buf.at[me], dst_ref=gram_buf.at[me],
            send_sem=g_send_sem.at[d - 1], recv_sem=g_recv_sem.at[d - 1],
            device_id={"space": lax.rem(me + d, space_count)}, device_id_type=MESH)
        copy.start()
        g_copies.append(copy)
    for copy in g_copies:
        copy.wait_recv()
    gram = gram_buf[0]
    for d in range(1, space_count):
        gram = gram + gram_buf[d]
    gram_ref[...] = gram

    for copy in copies + g_copies:
        copy.wait_send()


def modes_kernel(space_count, values, gram_ref, modes_hbm, factor_hbm, modes_vmem, factor_ref, modes_sem, factor_sem):
    columns, variables, freq, cells = values.shape
    pairs = [(i, j) for i in range(columns) for j in range(i + 1)]
    lane = lax.broadcasted_iota(jnp.int32, (freq, 128), 1)
    gram = gram_ref[...] * (1.0 / (variables * cells * space_count))
    entry = {
        pair: jnp.broadcast_to(gram[:, n:n + 1], (freq, 128)) for n, pair in enumerate(pairs)}

    lower, inverse = {}, {}
    for j in range(columns):
        rest = entry[j, j]
        for k in range(j):
            rest = rest - lower[j, k] * lower[j, k]
        inverse[j, j] = lax.rsqrt(rest)
        lower[j, j] = rest * inverse[j, j]
        for i in range(j + 1, columns):
            rest = entry[i, j]
            for k in range(j):
                rest = rest - lower[i, k] * lower[j, k]
            lower[i, j] = rest * inverse[j, j]
    for j in range(columns):
        for i in range(j + 1, columns):
            total = lower[i, j] * inverse[j, j]
            for k in range(j + 1, i):
                total = total + lower[i, k] * inverse[k, j]
            inverse[i, j] = -total * inverse[i, i]

    for i in range(columns):
        line = jnp.zeros((freq, 128), jnp.float32)
        for j in range(i, columns):
            line = jnp.where(lane == j, lower[j, i], line)
        factor_ref[i] = line[:, :columns]

    copies = [pltpu.make_async_copy(factor_ref, factor_hbm, factor_sem)]
    copies[0].start()
    for i in range(columns):
        for v in range(variables):
            for at in range(0, cells, 128):
                one = pl.ds(at, 128)
                mode = inverse[i, 0] * values[0, v, :, one]
                for j in range(1, i + 1):
                    mode = mode + inverse[i, j] * values[j, v, :, one]
                modes_vmem[i, v, :, one] = mode
        copy = pltpu.make_async_copy(modes_vmem.at[i], modes_hbm.at[i], modes_sem.at[i])
        copy.start()
        copies.append(copy)
    for copy in copies:
        copy.wait()


def on_device_kernel(snapshots, weights, bins):
    frames, variables, cells = snapshots.shape
    space_count = lax.axis_size("space")
    freq, columns = 8, 6
    rows = 2 * freq
    dma = pltpu.SemaphoreType.DMA
    inputs = [jnp.transpose(snapshots, (1, 0, 2)), weights, bins]
    inputs = [pltpu.with_memory_space_constraint(value, pltpu.HBM) for value in inputs]
    values, gram = pl.pallas_call(
        functools.partial(kernel, space_count, lax.axis_size("var")),
        out_shape=(
            jax.ShapeDtypeStruct((columns, variables, freq, cells), jnp.float32),
            jax.ShapeDtypeStruct((freq, 128), jnp.float32),
        ),
        in_specs=[
            pl.BlockSpec(memory_space=pltpu.HBM),
            pl.BlockSpec(memory_space=pltpu.HBM),
            pl.BlockSpec(memory_space=pltpu.HBM),
        ],
        out_specs=(pl.BlockSpec(memory_space=pltpu.VMEM),) * 2,
        scratch_shapes=[
            pltpu.VMEM((variables, frames, cells), jnp.bfloat16),
            pltpu.VMEM((variables, cells), jnp.float32),
            pltpu.SMEM(bins.shape, jnp.int32),
            pltpu.VMEM((variables, rows, cells), jnp.float32),
            pltpu.VMEM((variables, 2 * rows, cells), jnp.bfloat16),
            pltpu.VMEM((variables, 2 * rows, cells), jnp.bfloat16),
            pltpu.VMEM((space_count, freq, 128), jnp.float32),
            dma((variables,)), dma, dma,
            dma((variables,)), dma((variables,)),
            dma((space_count - 1,)), dma((space_count - 1,)),
        ],
        compiler_params=pltpu.CompilerParams(
            collective_id=0, has_side_effects=True, vmem_limit_bytes=32 * 1024 * 1024),
    )(*inputs)
    modes, factor = pl.pallas_call(
        functools.partial(modes_kernel, space_count),
        out_shape=(
            jax.ShapeDtypeStruct((columns, variables, freq, cells), jnp.float32),
            jax.ShapeDtypeStruct((columns, freq, columns), jnp.float32),
        ),
        in_specs=[pl.BlockSpec(memory_space=pltpu.VMEM)] * 2,
        out_specs=(pl.BlockSpec(memory_space=pltpu.HBM),) * 2,
        scratch_shapes=[
            pltpu.VMEM((columns, variables, freq, cells), jnp.float32),
            pltpu.VMEM((columns, freq, columns), jnp.float32),
            dma((columns,)), dma,
        ],
        compiler_params=pltpu.CompilerParams(vmem_limit_bytes=16 * 1024 * 1024),
    )(values, gram)
    return jnp.transpose(modes, (2, 0, 1, 3)), jnp.transpose(factor, (1, 0, 2))


def on_device(snapshots, weights, bins):
    seg_count = lax.axis_size("seg")
    var_count = lax.axis_size("var")
    space_count = lax.axis_size("space")
    frames, variables, cell_dev = snapshots.shape
    flat_rows = variables * cell_dev
    hop_len = frames // 2
    block_count = 2 * seg_count - 1
    freq_dev = bins.shape[0] // (seg_count * var_count)
    own = snapshots.reshape(frames, flat_rows)
    start_bin = (lax.axis_index("seg") * var_count + lax.axis_index("var")) * freq_dev
    chosen = lax.dynamic_slice_in_dim(bins, start_bin, freq_dev)
    piece = lax.all_gather(own, "seg", axis=0, tiled=True)
    count = piece.shape[0]
    moments = jnp.arange(count, dtype=jnp.int32)
    offset = moments[:, None] - hop_len * jnp.arange(block_count, dtype=jnp.int32)[None, :]
    inside = (offset >= 0) & (offset < frames)
    safe_offset = jnp.where(inside, offset, 0)
    cosine, sine = window_basis(safe_offset[:, :, None], chosen[None, None, :], frames)
    coeffs = jnp.stack([cosine, sine], 3) * inside[:, :, None, None].astype(jnp.float32)
    coeffs = jnp.transpose(coeffs, (0, 2, 3, 1)).reshape(count, freq_dev * 2 * block_count)
    coeffs = coeffs.astype(jnp.bfloat16)
    summed = jnp.einsum("pk,pr->kr", coeffs, piece, preferred_element_type=jnp.float32)
    spectra = summed.astype(jnp.bfloat16).reshape(freq_dev, 2 * block_count, flat_rows)
    values = spectra.astype(jnp.float32)
    scaled = values * weights.reshape(flat_rows)
    local_gram = jnp.einsum("fir,fjr->fij", scaled, values, precision=lax.Precision.HIGHEST)
    local_gram = local_gram / (variables * cell_dev * space_count)
    lower = jnp.linalg.cholesky(lax.psum(local_gram, "space"))
    inverse = invert_lower(lower)
    modes = jnp.einsum("fij,fjr->fir", inverse, values, precision=lax.Precision.HIGHEST)
    modes = modes.reshape(freq_dev, 2 * block_count, variables, cell_dev)
    return (modes, jnp.swapaxes(lower, 1, 2))


def per_device(snapshots, weights, bins):
    seg_count = lax.axis_size("seg")
    frames, variables, cells = snapshots.shape
    freq_dev = bins.shape[0] // (seg_count * lax.axis_size("var"))
    fits = seg_count == 2 and lax.axis_size("var") == 2 and freq_dev == 8 and cells % 128 == 0
    fits = fits and frames >= 256 and frames & (frames - 1) == 0 and lax.axis_size("space") > 1
    return (on_device_kernel if fits else on_device)(snapshots, weights, bins)


def solution(mesh):
    return jax.shard_map(
        per_device,
        mesh=mesh,
        in_specs=(P(("grp", "seg"), None, "space"), P(None, ("grp", "space")), P()),
        out_specs=(
            P(("seg", "var"), None, None, ("grp", "space")),
            P(("grp", "seg", "var"), None, None),
        ),
        check_vma=False,
    )
```

```python
import functools
import math

import jax
import jax.numpy as jnp
from jax import lax
from jax.experimental import pallas as pl
from jax.experimental.pallas import tpu as pltpu
from jax.sharding import PartitionSpec as P


def window_basis(offset, bin_index, length):
    phase = offset * bin_index % length
    angle = 2.0 * math.pi / length * phase.astype(jnp.float32)
    taper = 0.5 - 0.5 * jnp.cos(2.0 * math.pi / length * offset.astype(jnp.float32))
    factor = taper / math.sqrt(0.375 * length)
    return (factor * jnp.cos(angle), -factor * jnp.sin(angle))


def invert_lower(lower):
    identity = jnp.eye(lower.shape[-1], dtype=lower.dtype)

    def solve_single(single):
        return jax.scipy.linalg.solve_triangular(single, identity, lower=True)

    return jax.vmap(solve_single)(lower)


MESH = pl.DeviceIdType.MESH


def cosine_of(phase, length):
    quarter = jnp.abs(phase - length // 2) - length // 4
    x = quarter.astype(jnp.float32) * (2.0 * math.pi / length)
    y = x * x
    poly = -1.0 / 39916800.0
    for term in (1.0 / 362880.0, -1.0 / 5040.0, 1.0 / 120.0, -1.0 / 6.0, 1.0):
        poly = poly * y + term
    return x * poly


def basis_rows(bins_ref, frames, seg, var, var_count):
    freq = 8
    shape = (freq, frames)
    frame = lax.broadcasted_iota(jnp.int32, shape, 1)
    row = lax.broadcasted_iota(jnp.int32, shape, 0)
    half = frames // 2
    taper = (0.5 - 0.5 * cosine_of(frame, frames)) / math.sqrt(0.375 * frames)
    second = (lax.broadcasted_iota(jnp.int32, (2 * freq, frames), 1) >= half).astype(jnp.int32)
    overlap = second == 1 - seg
    rows = []
    for group in range(2):
        owner = 1 - seg if group == 0 else seg
        first = (owner * var_count + var) * freq
        bin_of = jnp.zeros(shape, jnp.int32)
        for f in range(freq):
            bin_of = jnp.where(row == f, bins_ref[first + f], bin_of)
        phase = (frame * bin_of) & (frames - 1)
        cosine = taper * cosine_of(phase, frames)
        sine = taper * cosine_of((phase + frames // 4) & (frames - 1), frames)
        whole = jnp.concatenate([cosine, sine], 0)
        shared = jnp.concatenate([whole[:, half:], whole[:, :half]], 1)
        rows += [whole, jnp.where(overlap, shared, 0.0)]
    return jnp.concatenate(rows, 0).astype(jnp.bfloat16)


def kernel(space_count, var_count, x_hbm, w_hbm, bins_hbm, values, gram_ref,
           x_vmem, w_ref, bins_ref, own_half, send, recv, gram_buf,
           x_sem, w_sem, bins_sem, send_sem, recv_sem, g_send_sem, g_recv_sem, turn_sem):
    variables, frames, cells = x_hbm.shape
    freq = 8
    rows = 2 * freq
    seg = lax.axis_index("seg")
    var = lax.axis_index("var")
    me = lax.axis_index("space")
    other = 1 - seg
    bins_load = pltpu.make_async_copy(bins_hbm, bins_ref, bins_sem)
    bins_load.start()
    loads = []
    for v in range(variables):
        load = pltpu.make_async_copy(x_hbm.at[v], x_vmem.at[v], x_sem.at[v])
        load.start()
        loads.append(load)

    w_load = pltpu.make_async_copy(w_hbm, w_ref, w_sem)
    w_load.start()

    barrier = pltpu.get_barrier_semaphore()
    pl.semaphore_signal(barrier, inc=1, device_id={"seg": other}, device_id_type=MESH)
    pl.semaphore_signal(barrier, inc=1, device_id={"var": 1 - var}, device_id_type=MESH)
    for d in range(1, space_count):
        pl.semaphore_signal(
            barrier, inc=1, device_id={"space": lax.rem(me + d, space_count)}, device_id_type=MESH)

    bins_load.wait()
    basis = basis_rows(bins_ref, frames, seg, var, var_count)
    pl.semaphore_wait(barrier, space_count + 1)

    copies = []
    for v in range(variables):
        loads[v].wait()
        summed = jnp.dot(basis, x_vmem[v], preferred_element_type=jnp.float32)
        send[v] = summed[:2 * rows].astype(send.dtype)
        copy = pltpu.make_async_remote_copy(
            src_ref=send.at[v], dst_ref=recv.at[v], send_sem=send_sem.at[v], recv_sem=recv_sem.at[v],
            device_id={"seg": other}, device_id_type=MESH)
        pl.when(var == 0)(copy.start)
        copies.append(copy)
        own = summed[2 * rows:3 * rows].astype(jnp.bfloat16).astype(jnp.float32)
        own_half[v] = summed[3 * rows:]
        for part in range(2):
            values[3 * part + 2 * seg, v] = own[part * freq:(part + 1) * freq]

    @pl.when(var == 0)
    def _():
        pl.semaphore_signal(turn_sem, inc=1, device_id={"var": 1 - var}, device_id_type=MESH)

    @pl.when(var != 0)
    def _():
        pl.semaphore_wait(turn_sem, 1)
        for copy in copies:
            copy.start()

    w_load.wait()
    columns = 6
    pairs = [(i, j) for i in range(columns) for j in range(i + 1)]
    sums = [None] * len(pairs)
    for v in range(variables):
        copies[v].wait_recv()
        far = recv[v].astype(jnp.float32)
        total = own_half[v] + far[rows:]
        total = total.astype(jnp.bfloat16).astype(jnp.float32)
        for part in range(2):
            values[3 * part + 1, v] = total[part * freq:(part + 1) * freq]
            values[3 * part + 2 * other, v] = far[part * freq:(part + 1) * freq]
        for at in range(0, cells, 128):
            one = pl.ds(at, 128)
            weight = jnp.broadcast_to(w_ref[v:v + 1, one], (freq, 128))
            plain = [values[i, v, :, one] for i in range(columns)]
            scaled = [p * weight for p in plain]
            for n, (i, j) in enumerate(pairs):
                term = scaled[i] * plain[j]
                sums[n] = term if sums[n] is None else sums[n] + term

    lane = lax.broadcasted_iota(jnp.int32, (freq, 128), 1)
    packed = jnp.zeros((freq, 128), jnp.float32)
    for n in range(len(pairs)):
        packed = jnp.where(lane == n, jnp.sum(sums[n], axis=1, keepdims=True), packed)
    gram_buf[me] = packed
    g_copies = []
    for d in range(1, space_count):
        copy = pltpu.make_async_remote_copy(
            src_ref=gram_buf.at[me], dst_ref=gram_buf.at[me],
            send_sem=g_send_sem.at[d - 1], recv_sem=g_recv_sem.at[d - 1],
            device_id={"space": lax.rem(me + d, space_count)}, device_id_type=MESH)
        copy.start()
        g_copies.append(copy)
    for copy in g_copies:
        copy.wait_recv()
    gram = gram_buf[0]
    for d in range(1, space_count):
        gram = gram + gram_buf[d]
    gram_ref[...] = gram

    for copy in copies + g_copies:
        copy.wait_send()


def modes_kernel(space_count, values, gram_ref, modes_hbm, factor_hbm, modes_vmem, factor_ref, modes_sem, factor_sem):
    columns, variables, freq, cells = values.shape
    pairs = [(i, j) for i in range(columns) for j in range(i + 1)]
    lane = lax.broadcasted_iota(jnp.int32, (freq, 128), 1)
    gram = gram_ref[...] * (1.0 / (variables * cells * space_count))
    entry = {
        pair: jnp.broadcast_to(gram[:, n:n + 1], (freq, 128)) for n, pair in enumerate(pairs)}

    lower, inverse = {}, {}
    for j in range(columns):
        rest = entry[j, j]
        for k in range(j):
            rest = rest - lower[j, k] * lower[j, k]
        inverse[j, j] = lax.rsqrt(rest)
        lower[j, j] = rest * inverse[j, j]
        for i in range(j + 1, columns):
            rest = entry[i, j]
            for k in range(j):
                rest = rest - lower[i, k] * lower[j, k]
            lower[i, j] = rest * inverse[j, j]
    for j in range(columns):
        for i in range(j + 1, columns):
            total = lower[i, j] * inverse[j, j]
            for k in range(j + 1, i):
                total = total + lower[i, k] * inverse[k, j]
            inverse[i, j] = -total * inverse[i, i]

    for i in range(columns):
        line = jnp.zeros((freq, 128), jnp.float32)
        for j in range(i, columns):
            line = jnp.where(lane == j, lower[j, i], line)
        factor_ref[i] = line[:, :columns]

    copies = [pltpu.make_async_copy(factor_ref, factor_hbm, factor_sem)]
    copies[0].start()
    for i in range(columns):
        for v in range(variables):
            for at in range(0, cells, 128):
                one = pl.ds(at, 128)
                mode = inverse[i, 0] * values[0, v, :, one]
                for j in range(1, i + 1):
                    mode = mode + inverse[i, j] * values[j, v, :, one]
                modes_vmem[i, v, :, one] = mode
        copy = pltpu.make_async_copy(modes_vmem.at[i], modes_hbm.at[i], modes_sem.at[i])
        copy.start()
        copies.append(copy)
    for copy in copies:
        copy.wait()


def on_device_kernel(snapshots, weights, bins):
    frames, variables, cells = snapshots.shape
    space_count = lax.axis_size("space")
    freq, columns = 8, 6
    rows = 2 * freq
    dma = pltpu.SemaphoreType.DMA
    inputs = [jnp.transpose(snapshots, (1, 0, 2)), weights, bins]
    inputs = [pltpu.with_memory_space_constraint(value, pltpu.HBM) for value in inputs]
    values, gram = pl.pallas_call(
        functools.partial(kernel, space_count, lax.axis_size("var")),
        out_shape=(
            jax.ShapeDtypeStruct((columns, variables, freq, cells), jnp.float32),
            jax.ShapeDtypeStruct((freq, 128), jnp.float32),
        ),
        in_specs=[
            pl.BlockSpec(memory_space=pltpu.HBM),
            pl.BlockSpec(memory_space=pltpu.HBM),
            pl.BlockSpec(memory_space=pltpu.HBM),
        ],
        out_specs=(pl.BlockSpec(memory_space=pltpu.VMEM),) * 2,
        scratch_shapes=[
            pltpu.VMEM((variables, frames, cells), jnp.bfloat16),
            pltpu.VMEM((variables, cells), jnp.float32),
            pltpu.SMEM(bins.shape, jnp.int32),
            pltpu.VMEM((variables, rows, cells), jnp.float32),
            pltpu.VMEM((variables, 2 * rows, cells), jnp.bfloat16),
            pltpu.VMEM((variables, 2 * rows, cells), jnp.bfloat16),
            pltpu.VMEM((space_count, freq, 128), jnp.float32),
            dma((variables,)), dma, dma,
            dma((variables,)), dma((variables,)),
            dma((space_count - 1,)), dma((space_count - 1,)),
            pltpu.SemaphoreType.REGULAR,
        ],
        compiler_params=pltpu.CompilerParams(
            collective_id=0, has_side_effects=True, vmem_limit_bytes=32 * 1024 * 1024),
    )(*inputs)
    modes, factor = pl.pallas_call(
        functools.partial(modes_kernel, space_count),
        out_shape=(
            jax.ShapeDtypeStruct((columns, variables, freq, cells), jnp.float32),
            jax.ShapeDtypeStruct((columns, freq, columns), jnp.float32),
        ),
        in_specs=[pl.BlockSpec(memory_space=pltpu.VMEM)] * 2,
        out_specs=(pl.BlockSpec(memory_space=pltpu.HBM),) * 2,
        scratch_shapes=[
            pltpu.VMEM((columns, variables, freq, cells), jnp.float32),
            pltpu.VMEM((columns, freq, columns), jnp.float32),
            dma((columns,)), dma,
        ],
        compiler_params=pltpu.CompilerParams(vmem_limit_bytes=16 * 1024 * 1024),
    )(values, gram)
    return jnp.transpose(modes, (2, 0, 1, 3)), jnp.transpose(factor, (1, 0, 2))


def on_device(snapshots, weights, bins):
    seg_count = lax.axis_size("seg")
    var_count = lax.axis_size("var")
    space_count = lax.axis_size("space")
    frames, variables, cell_dev = snapshots.shape
    flat_rows = variables * cell_dev
    hop_len = frames // 2
    block_count = 2 * seg_count - 1
    freq_dev = bins.shape[0] // (seg_count * var_count)
    own = snapshots.reshape(frames, flat_rows)
    start_bin = (lax.axis_index("seg") * var_count + lax.axis_index("var")) * freq_dev
    chosen = lax.dynamic_slice_in_dim(bins, start_bin, freq_dev)
    piece = lax.all_gather(own, "seg", axis=0, tiled=True)
    count = piece.shape[0]
    moments = jnp.arange(count, dtype=jnp.int32)
    offset = moments[:, None] - hop_len * jnp.arange(block_count, dtype=jnp.int32)[None, :]
    inside = (offset >= 0) & (offset < frames)
    safe_offset = jnp.where(inside, offset, 0)
    cosine, sine = window_basis(safe_offset[:, :, None], chosen[None, None, :], frames)
    coeffs = jnp.stack([cosine, sine], 3) * inside[:, :, None, None].astype(jnp.float32)
    coeffs = jnp.transpose(coeffs, (0, 2, 3, 1)).reshape(count, freq_dev * 2 * block_count)
    coeffs = coeffs.astype(jnp.bfloat16)
    summed = jnp.einsum("pk,pr->kr", coeffs, piece, preferred_element_type=jnp.float32)
    spectra = summed.astype(jnp.bfloat16).reshape(freq_dev, 2 * block_count, flat_rows)
    values = spectra.astype(jnp.float32)
    scaled = values * weights.reshape(flat_rows)
    local_gram = jnp.einsum("fir,fjr->fij", scaled, values, precision=lax.Precision.HIGHEST)
    local_gram = local_gram / (variables * cell_dev * space_count)
    lower = jnp.linalg.cholesky(lax.psum(local_gram, "space"))
    inverse = invert_lower(lower)
    modes = jnp.einsum("fij,fjr->fir", inverse, values, precision=lax.Precision.HIGHEST)
    modes = modes.reshape(freq_dev, 2 * block_count, variables, cell_dev)
    return (modes, jnp.swapaxes(lower, 1, 2))


def per_device(snapshots, weights, bins):
    seg_count = lax.axis_size("seg")
    frames, variables, cells = snapshots.shape
    freq_dev = bins.shape[0] // (seg_count * lax.axis_size("var"))
    fits = seg_count == 2 and lax.axis_size("var") == 2 and freq_dev == 8 and cells % 128 == 0
    fits = fits and frames >= 256 and frames & (frames - 1) == 0 and lax.axis_size("space") > 1
    return (on_device_kernel if fits else on_device)(snapshots, weights, bins)


def solution(mesh):
    return jax.shard_map(
        per_device,
        mesh=mesh,
        in_specs=(P(("grp", "seg"), None, "space"), P(None, ("grp", "space")), P()),
        out_specs=(
            P(("seg", "var"), None, None, ("grp", "space")),
            P(("grp", "seg", "var"), None, None),
        ),
        check_vma=False,
    )
```

```python
import functools
import math

import jax
import jax.numpy as jnp
from jax import lax
from jax.experimental import pallas as pl
from jax.experimental.pallas import tpu as pltpu
from jax.sharding import PartitionSpec as P


def window_basis(offset, bin_index, length):
    phase = offset * bin_index % length
    angle = 2.0 * math.pi / length * phase.astype(jnp.float32)
    taper = 0.5 - 0.5 * jnp.cos(2.0 * math.pi / length * offset.astype(jnp.float32))
    factor = taper / math.sqrt(0.375 * length)
    return (factor * jnp.cos(angle), -factor * jnp.sin(angle))


def invert_lower(lower):
    identity = jnp.eye(lower.shape[-1], dtype=lower.dtype)

    def solve_single(single):
        return jax.scipy.linalg.solve_triangular(single, identity, lower=True)

    return jax.vmap(solve_single)(lower)


MESH = pl.DeviceIdType.MESH


def cosine_of(phase, length):
    quarter = jnp.abs(phase - length // 2) - length // 4
    x = quarter.astype(jnp.float32) * (2.0 * math.pi / length)
    y = x * x
    poly = -1.0 / 39916800.0
    for term in (1.0 / 362880.0, -1.0 / 5040.0, 1.0 / 120.0, -1.0 / 6.0, 1.0):
        poly = poly * y + term
    return x * poly


def basis_rows(bins_ref, frames, seg, var, var_count):
    freq = 8
    shape = (freq, frames)
    frame = lax.broadcasted_iota(jnp.int32, shape, 1)
    row = lax.broadcasted_iota(jnp.int32, shape, 0)
    half = frames // 2
    taper = (0.5 - 0.5 * cosine_of(frame, frames)) / math.sqrt(0.375 * frames)
    second = (lax.broadcasted_iota(jnp.int32, (2 * freq, frames), 1) >= half).astype(jnp.int32)
    overlap = second == 1 - seg
    rows = []
    for group in range(2):
        owner = 1 - seg if group == 0 else seg
        first = (owner * var_count + var) * freq
        bin_of = jnp.zeros(shape, jnp.int32)
        for f in range(freq):
            bin_of = jnp.where(row == f, bins_ref[first + f], bin_of)
        phase = (frame * bin_of) & (frames - 1)
        cosine = taper * cosine_of(phase, frames)
        sine = taper * cosine_of((phase + frames // 4) & (frames - 1), frames)
        whole = jnp.concatenate([cosine, sine], 0)
        shared = jnp.concatenate([whole[:, half:], whole[:, :half]], 1)
        rows += [whole, jnp.where(overlap, shared, 0.0)]
    return jnp.concatenate(rows, 0).astype(jnp.bfloat16)


def kernel(space_count, var_count, x_hbm, w_hbm, bins_hbm, values, gram_ref,
           x_vmem, w_ref, bins_ref, own_half, send, recv, gram_buf,
           x_sem, w_sem, bins_sem, send_sem, recv_sem, g_send_sem, g_recv_sem, turn_sem):
    variables, frames, cells = x_hbm.shape
    freq = 8
    rows = 2 * freq
    seg = lax.axis_index("seg")
    var = lax.axis_index("var")
    me = lax.axis_index("space")
    other = 1 - seg
    bins_load = pltpu.make_async_copy(bins_hbm, bins_ref, bins_sem)
    bins_load.start()
    loads = []
    for v in range(variables):
        load = pltpu.make_async_copy(x_hbm.at[v], x_vmem.at[v], x_sem.at[v])
        load.start()
        loads.append(load)

    w_load = pltpu.make_async_copy(w_hbm, w_ref, w_sem)
    w_load.start()

    barrier = pltpu.get_barrier_semaphore()
    pl.semaphore_signal(barrier, inc=1, device_id={"seg": other}, device_id_type=MESH)
    pl.semaphore_signal(barrier, inc=1, device_id={"var": 1 - var}, device_id_type=MESH)
    for d in range(1, space_count):
        pl.semaphore_signal(
            barrier, inc=1, device_id={"space": lax.rem(me + d, space_count)}, device_id_type=MESH)

    bins_load.wait()
    basis = basis_rows(bins_ref, frames, seg, var, var_count)

    pl.semaphore_wait(barrier, space_count + 1)
    early = 2
    copies = [
        pltpu.make_async_remote_copy(
            src_ref=send.at[v], dst_ref=recv.at[v], send_sem=send_sem.at[v], recv_sem=recv_sem.at[v],
            device_id={"seg": other}, device_id_type=MESH)
        for v in range(variables)]

    def transform(v):
        loads[v].wait()
        summed = jnp.dot(basis, x_vmem[v], preferred_element_type=jnp.float32)
        send[v] = summed[:2 * rows].astype(send.dtype)
        own = summed[2 * rows:3 * rows].astype(jnp.bfloat16).astype(jnp.float32)
        own_half[v] = summed[3 * rows:]
        for part in range(2):
            values[3 * part + 2 * seg, v] = own[part * freq:(part + 1) * freq]

    @pl.when(var == 0)
    def _():
        for v in range(variables):
            transform(v)
            copies[v].start()
        for copy in copies[:early]:
            copy.wait_send()
        pl.semaphore_signal(turn_sem, inc=1, device_id={"var": 1 - var}, device_id_type=MESH)

    @pl.when(var != 0)
    def _():
        for v in range(variables):
            transform(v)
        pl.semaphore_wait(turn_sem, 1)
        for copy in copies:
            copy.start()

    w_load.wait()
    columns = 6
    pairs = [(i, j) for i in range(columns) for j in range(i + 1)]
    sums = [None] * len(pairs)
    for v in range(variables):
        copies[v].wait_recv()
        far = recv[v].astype(jnp.float32)
        total = own_half[v] + far[rows:]
        total = total.astype(jnp.bfloat16).astype(jnp.float32)
        for part in range(2):
            values[3 * part + 1, v] = total[part * freq:(part + 1) * freq]
            values[3 * part + 2 * other, v] = far[part * freq:(part + 1) * freq]
        for at in range(0, cells, 128):
            one = pl.ds(at, 128)
            weight = jnp.broadcast_to(w_ref[v:v + 1, one], (freq, 128))
            plain = [values[i, v, :, one] for i in range(columns)]
            scaled = [p * weight for p in plain]
            for n, (i, j) in enumerate(pairs):
                term = scaled[i] * plain[j]
                sums[n] = term if sums[n] is None else sums[n] + term

    lane = lax.broadcasted_iota(jnp.int32, (freq, 128), 1)
    packed = jnp.zeros((freq, 128), jnp.float32)
    for n in range(len(pairs)):
        packed = jnp.where(lane == n, jnp.sum(sums[n], axis=1, keepdims=True), packed)
    gram_buf[me] = packed
    g_copies = []
    for d in range(1, space_count):
        copy = pltpu.make_async_remote_copy(
            src_ref=gram_buf.at[me], dst_ref=gram_buf.at[me],
            send_sem=g_send_sem.at[d - 1], recv_sem=g_recv_sem.at[d - 1],
            device_id={"space": lax.rem(me + d, space_count)}, device_id_type=MESH)
        copy.start()
        g_copies.append(copy)
    for copy in g_copies:
        copy.wait_recv()
    gram = gram_buf[0]
    for d in range(1, space_count):
        gram = gram + gram_buf[d]
    gram_ref[...] = gram

    @pl.when(var != 0)
    def _():
        for copy in copies[:early]:
            copy.wait_send()

    for copy in copies[early:] + g_copies:
        copy.wait_send()


def modes_kernel(space_count, values, gram_ref, modes_hbm, factor_hbm, modes_vmem, factor_ref, modes_sem, factor_sem):
    columns, variables, freq, cells = values.shape
    pairs = [(i, j) for i in range(columns) for j in range(i + 1)]
    lane = lax.broadcasted_iota(jnp.int32, (freq, 128), 1)
    gram = gram_ref[...] * (1.0 / (variables * cells * space_count))
    entry = {
        pair: jnp.broadcast_to(gram[:, n:n + 1], (freq, 128)) for n, pair in enumerate(pairs)}

    lower, inverse = {}, {}
    for j in range(columns):
        rest = entry[j, j]
        for k in range(j):
            rest = rest - lower[j, k] * lower[j, k]
        inverse[j, j] = lax.rsqrt(rest)
        lower[j, j] = rest * inverse[j, j]
        for i in range(j + 1, columns):
            rest = entry[i, j]
            for k in range(j):
                rest = rest - lower[i, k] * lower[j, k]
            lower[i, j] = rest * inverse[j, j]
    for j in range(columns):
        for i in range(j + 1, columns):
            total = lower[i, j] * inverse[j, j]
            for k in range(j + 1, i):
                total = total + lower[i, k] * inverse[k, j]
            inverse[i, j] = -total * inverse[i, i]

    for i in range(columns):
        line = jnp.zeros((freq, 128), jnp.float32)
        for j in range(i, columns):
            line = jnp.where(lane == j, lower[j, i], line)
        factor_ref[i] = line[:, :columns]

    copies = [pltpu.make_async_copy(factor_ref, factor_hbm, factor_sem)]
    copies[0].start()
    for i in range(columns):
        for v in range(variables):
            for at in range(0, cells, 128):
                one = pl.ds(at, 128)
                mode = inverse[i, 0] * values[0, v, :, one]
                for j in range(1, i + 1):
                    mode = mode + inverse[i, j] * values[j, v, :, one]
                modes_vmem[i, v, :, one] = mode
        copy = pltpu.make_async_copy(modes_vmem.at[i], modes_hbm.at[i], modes_sem.at[i])
        copy.start()
        copies.append(copy)
    for copy in copies:
        copy.wait()


def on_device_kernel(snapshots, weights, bins):
    frames, variables, cells = snapshots.shape
    space_count = lax.axis_size("space")
    freq, columns = 8, 6
    rows = 2 * freq
    dma = pltpu.SemaphoreType.DMA
    inputs = [jnp.transpose(snapshots, (1, 0, 2)), weights, bins]
    inputs = [pltpu.with_memory_space_constraint(value, pltpu.HBM) for value in inputs]
    values, gram = pl.pallas_call(
        functools.partial(kernel, space_count, lax.axis_size("var")),
        out_shape=(
            jax.ShapeDtypeStruct((columns, variables, freq, cells), jnp.float32),
            jax.ShapeDtypeStruct((freq, 128), jnp.float32),
        ),
        in_specs=[
            pl.BlockSpec(memory_space=pltpu.HBM),
            pl.BlockSpec(memory_space=pltpu.HBM),
            pl.BlockSpec(memory_space=pltpu.HBM),
        ],
        out_specs=(pl.BlockSpec(memory_space=pltpu.VMEM),) * 2,
        scratch_shapes=[
            pltpu.VMEM((variables, frames, cells), jnp.bfloat16),
            pltpu.VMEM((variables, cells), jnp.float32),
            pltpu.SMEM(bins.shape, jnp.int32),
            pltpu.VMEM((variables, rows, cells), jnp.float32),
            pltpu.VMEM((variables, 2 * rows, cells), jnp.bfloat16),
            pltpu.VMEM((variables, 2 * rows, cells), jnp.bfloat16),
            pltpu.VMEM((space_count, freq, 128), jnp.float32),
            dma((variables,)), dma, dma,
            dma((variables,)), dma((variables,)),
            dma((space_count - 1,)), dma((space_count - 1,)),
            pltpu.SemaphoreType.REGULAR,
        ],
        compiler_params=pltpu.CompilerParams(
            collective_id=0, has_side_effects=True, vmem_limit_bytes=32 * 1024 * 1024),
    )(*inputs)
    modes, factor = pl.pallas_call(
        functools.partial(modes_kernel, space_count),
        out_shape=(
            jax.ShapeDtypeStruct((columns, variables, freq, cells), jnp.float32),
            jax.ShapeDtypeStruct((columns, freq, columns), jnp.float32),
        ),
        in_specs=[pl.BlockSpec(memory_space=pltpu.VMEM)] * 2,
        out_specs=(pl.BlockSpec(memory_space=pltpu.HBM),) * 2,
        scratch_shapes=[
            pltpu.VMEM((columns, variables, freq, cells), jnp.float32),
            pltpu.VMEM((columns, freq, columns), jnp.float32),
            dma((columns,)), dma,
        ],
        compiler_params=pltpu.CompilerParams(vmem_limit_bytes=16 * 1024 * 1024),
    )(values, gram)
    return jnp.transpose(modes, (2, 0, 1, 3)), jnp.transpose(factor, (1, 0, 2))


def on_device(snapshots, weights, bins):
    seg_count = lax.axis_size("seg")
    var_count = lax.axis_size("var")
    space_count = lax.axis_size("space")
    frames, variables, cell_dev = snapshots.shape
    flat_rows = variables * cell_dev
    hop_len = frames // 2
    block_count = 2 * seg_count - 1
    freq_dev = bins.shape[0] // (seg_count * var_count)
    own = snapshots.reshape(frames, flat_rows)
    start_bin = (lax.axis_index("seg") * var_count + lax.axis_index("var")) * freq_dev
    chosen = lax.dynamic_slice_in_dim(bins, start_bin, freq_dev)
    piece = lax.all_gather(own, "seg", axis=0, tiled=True)
    count = piece.shape[0]
    moments = jnp.arange(count, dtype=jnp.int32)
    offset = moments[:, None] - hop_len * jnp.arange(block_count, dtype=jnp.int32)[None, :]
    inside = (offset >= 0) & (offset < frames)
    safe_offset = jnp.where(inside, offset, 0)
    cosine, sine = window_basis(safe_offset[:, :, None], chosen[None, None, :], frames)
    coeffs = jnp.stack([cosine, sine], 3) * inside[:, :, None, None].astype(jnp.float32)
    coeffs = jnp.transpose(coeffs, (0, 2, 3, 1)).reshape(count, freq_dev * 2 * block_count)
    coeffs = coeffs.astype(jnp.bfloat16)
    summed = jnp.einsum("pk,pr->kr", coeffs, piece, preferred_element_type=jnp.float32)
    spectra = summed.astype(jnp.bfloat16).reshape(freq_dev, 2 * block_count, flat_rows)
    values = spectra.astype(jnp.float32)
    scaled = values * weights.reshape(flat_rows)
    local_gram = jnp.einsum("fir,fjr->fij", scaled, values, precision=lax.Precision.HIGHEST)
    local_gram = local_gram / (variables * cell_dev * space_count)
    lower = jnp.linalg.cholesky(lax.psum(local_gram, "space"))
    inverse = invert_lower(lower)
    modes = jnp.einsum("fij,fjr->fir", inverse, values, precision=lax.Precision.HIGHEST)
    modes = modes.reshape(freq_dev, 2 * block_count, variables, cell_dev)
    return (modes, jnp.swapaxes(lower, 1, 2))


def per_device(snapshots, weights, bins):
    seg_count = lax.axis_size("seg")
    frames, variables, cells = snapshots.shape
    freq_dev = bins.shape[0] // (seg_count * lax.axis_size("var"))
    fits = seg_count == 2 and lax.axis_size("var") == 2 and freq_dev == 8 and cells % 128 == 0
    fits = fits and frames >= 256 and frames & (frames - 1) == 0 and lax.axis_size("space") > 1
    return (on_device_kernel if fits else on_device)(snapshots, weights, bins)


def solution(mesh):
    return jax.shard_map(
        per_device,
        mesh=mesh,
        in_specs=(P(("grp", "seg"), None, "space"), P(None, ("grp", "space")), P()),
        out_specs=(
            P(("seg", "var"), None, None, ("grp", "space")),
            P(("grp", "seg", "var"), None, None),
        ),
        check_vma=False,
    )
```

```python
import functools
import math

import jax
import jax.numpy as jnp
from jax import lax
from jax.experimental import pallas as pl
from jax.experimental.pallas import tpu as pltpu
from jax.sharding import PartitionSpec as P


def window_basis(offset, bin_index, length):
    phase = offset * bin_index % length
    angle = 2.0 * math.pi / length * phase.astype(jnp.float32)
    taper = 0.5 - 0.5 * jnp.cos(2.0 * math.pi / length * offset.astype(jnp.float32))
    factor = taper / math.sqrt(0.375 * length)
    return (factor * jnp.cos(angle), -factor * jnp.sin(angle))


def invert_lower(lower):
    identity = jnp.eye(lower.shape[-1], dtype=lower.dtype)

    def solve_single(single):
        return jax.scipy.linalg.solve_triangular(single, identity, lower=True)

    return jax.vmap(solve_single)(lower)


MESH = pl.DeviceIdType.MESH


def cosine_of(phase, length):
    quarter = jnp.abs(phase - length // 2) - length // 4
    x = quarter.astype(jnp.float32) * (2.0 * math.pi / length)
    y = x * x
    poly = -1.0 / 39916800.0
    for term in (1.0 / 362880.0, -1.0 / 5040.0, 1.0 / 120.0, -1.0 / 6.0, 1.0):
        poly = poly * y + term
    return x * poly


def basis_rows(bins_ref, frames, seg, var, var_count):
    freq = 8
    shape = (freq, frames)
    frame = lax.broadcasted_iota(jnp.int32, shape, 1)
    row = lax.broadcasted_iota(jnp.int32, shape, 0)
    half = frames // 2
    taper = (0.5 - 0.5 * cosine_of(frame, frames)) / math.sqrt(0.375 * frames)
    second = (lax.broadcasted_iota(jnp.int32, (2 * freq, frames), 1) >= half).astype(jnp.int32)
    overlap = second == 1 - seg
    rows = []
    for group in range(2):
        owner = 1 - seg if group == 0 else seg
        first = (owner * var_count + var) * freq
        bin_of = jnp.zeros(shape, jnp.int32)
        for f in range(freq):
            bin_of = jnp.where(row == f, bins_ref[first + f], bin_of)
        phase = (frame * bin_of) & (frames - 1)
        cosine = taper * cosine_of(phase, frames)
        sine = taper * cosine_of((phase + frames // 4) & (frames - 1), frames)
        whole = jnp.concatenate([cosine, sine], 0)
        shared = jnp.concatenate([whole[:, half:], whole[:, :half]], 1)
        rows += [whole, jnp.where(overlap, shared, 0.0)]
    return jnp.concatenate(rows, 0).astype(jnp.bfloat16)


def kernel(space_count, var_count, x_hbm, w_hbm, bins_hbm, values, gram_ref,
           x_vmem, w_ref, bins_ref, own_half, send, recv, gram_buf,
           x_sem, w_sem, bins_sem, send_sem, recv_sem, g_send_sem, g_recv_sem, turn_sem):
    variables, frames, cells = x_hbm.shape
    freq = 8
    rows = 2 * freq
    seg = lax.axis_index("seg")
    var = lax.axis_index("var")
    me = lax.axis_index("space")
    other = 1 - seg
    bins_load = pltpu.make_async_copy(bins_hbm, bins_ref, bins_sem)
    bins_load.start()
    for v in range(variables):
        pltpu.make_async_copy(x_hbm.at[v], x_vmem.at[v], x_sem.at[v]).start()

    w_load = pltpu.make_async_copy(w_hbm, w_ref, w_sem)
    w_load.start()

    barrier = pltpu.get_barrier_semaphore()
    pl.semaphore_signal(barrier, inc=1, device_id={"seg": other}, device_id_type=MESH)
    pl.semaphore_signal(barrier, inc=1, device_id={"var": 1 - var}, device_id_type=MESH)
    for d in range(1, space_count):
        pl.semaphore_signal(
            barrier, inc=1, device_id={"space": lax.rem(me + d, space_count)}, device_id_type=MESH)

    bins_load.wait()
    basis = basis_rows(bins_ref, frames, seg, var, var_count)

    pl.semaphore_wait(barrier, space_count + 1)
    early = 2
    copies = [
        pltpu.make_async_remote_copy(
            src_ref=send.at[v], dst_ref=recv.at[v], send_sem=send_sem.at[v], recv_sem=recv_sem.at[v],
            device_id={"seg": other}, device_id_type=MESH)
        for v in range(variables)]

    def transform(v):
        pltpu.make_async_copy(x_hbm.at[v], x_vmem.at[v], x_sem.at[v]).wait()
        summed = jnp.dot(basis, x_vmem[v], preferred_element_type=jnp.float32)
        send[v] = summed[:2 * rows].astype(send.dtype)
        own = summed[2 * rows:3 * rows].astype(jnp.bfloat16).astype(jnp.float32)
        own_half[v] = summed[3 * rows:]
        for part in range(2):
            values[3 * part + 2 * seg, v] = own[part * freq:(part + 1) * freq]

    @pl.when(var == 0)
    def _():
        for v in range(variables):
            transform(v)
            copies[v].start()
        for copy in copies[:early]:
            copy.wait_send()
        pl.semaphore_signal(turn_sem, inc=1, device_id={"var": 1 - var}, device_id_type=MESH)

    @pl.when(var != 0)
    def _():
        pl.loop(0, variables)(transform)
        pl.semaphore_wait(turn_sem, 1)
        for copy in copies:
            copy.start()

    w_load.wait()
    columns = 6
    pairs = [(i, j) for i in range(columns) for j in range(i + 1)]
    sums = tuple(jnp.zeros((freq, 128), jnp.float32) for _ in pairs)
    for v in range(variables):
        copies[v].wait_recv()
        far = recv[v].astype(jnp.float32)
        total = own_half[v] + far[rows:]
        total = total.astype(jnp.bfloat16).astype(jnp.float32)
        for part in range(2):
            values[3 * part + 1, v] = total[part * freq:(part + 1) * freq]
            values[3 * part + 2 * other, v] = far[part * freq:(part + 1) * freq]
        def add_block(block, sums, v=v):
            one = pl.ds(pl.multiple_of(block * 128, 128), 128)
            weight = jnp.broadcast_to(w_ref[v:v + 1, one], (freq, 128))
            plain = [values[i, v, :, one] for i in range(columns)]
            scaled = [p * weight for p in plain]
            return tuple(
                total + scaled[i] * plain[j] for total, (i, j) in zip(sums, pairs))

        sums = lax.fori_loop(0, cells // 128, add_block, sums)

    lane = lax.broadcasted_iota(jnp.int32, (freq, 128), 1)
    packed = jnp.zeros((freq, 128), jnp.float32)
    for n in range(len(pairs)):
        packed = jnp.where(lane == n, jnp.sum(sums[n], axis=1, keepdims=True), packed)
    gram_buf[me] = packed
    g_copies = []
    for d in range(1, space_count):
        copy = pltpu.make_async_remote_copy(
            src_ref=gram_buf.at[me], dst_ref=gram_buf.at[me],
            send_sem=g_send_sem.at[d - 1], recv_sem=g_recv_sem.at[d - 1],
            device_id={"space": lax.rem(me + d, space_count)}, device_id_type=MESH)
        copy.start()
        g_copies.append(copy)
    for copy in g_copies:
        copy.wait_recv()
    gram = gram_buf[0]
    for d in range(1, space_count):
        gram = gram + gram_buf[d]
    gram_ref[...] = gram

    @pl.when(var != 0)
    def _():
        for copy in copies[:early]:
            copy.wait_send()

    for copy in copies[early:] + g_copies:
        copy.wait_send()


def modes_kernel(space_count, values, gram_ref, modes_hbm, factor_hbm, modes_vmem, factor_ref, modes_sem, factor_sem):
    columns, variables, freq, cells = values.shape
    pairs = [(i, j) for i in range(columns) for j in range(i + 1)]
    lane = lax.broadcasted_iota(jnp.int32, (freq, 128), 1)
    gram = gram_ref[...] * (1.0 / (variables * cells * space_count))
    entry = {
        pair: jnp.broadcast_to(gram[:, n:n + 1], (freq, 128)) for n, pair in enumerate(pairs)}

    lower, inverse = {}, {}
    for j in range(columns):
        rest = entry[j, j]
        for k in range(j):
            rest = rest - lower[j, k] * lower[j, k]
        inverse[j, j] = lax.rsqrt(rest)
        lower[j, j] = rest * inverse[j, j]
        for i in range(j + 1, columns):
            rest = entry[i, j]
            for k in range(j):
                rest = rest - lower[i, k] * lower[j, k]
            lower[i, j] = rest * inverse[j, j]
    for j in range(columns):
        for i in range(j + 1, columns):
            total = lower[i, j] * inverse[j, j]
            for k in range(j + 1, i):
                total = total + lower[i, k] * inverse[k, j]
            inverse[i, j] = -total * inverse[i, i]

    for i in range(columns):
        line = jnp.zeros((freq, 128), jnp.float32)
        for j in range(i, columns):
            line = jnp.where(lane == j, lower[j, i], line)
        factor_ref[i] = line[:, :columns]

    copies = [pltpu.make_async_copy(factor_ref, factor_hbm, factor_sem)]
    copies[0].start()
    for i in range(columns):
        for v in range(variables):
            for at in range(0, cells, 128):
                one = pl.ds(at, 128)
                mode = inverse[i, 0] * values[0, v, :, one]
                for j in range(1, i + 1):
                    mode = mode + inverse[i, j] * values[j, v, :, one]
                modes_vmem[i, v, :, one] = mode
        copy = pltpu.make_async_copy(modes_vmem.at[i], modes_hbm.at[i], modes_sem.at[i])
        copy.start()
        copies.append(copy)
    for copy in copies:
        copy.wait()


def on_device_kernel(snapshots, weights, bins):
    frames, variables, cells = snapshots.shape
    space_count = lax.axis_size("space")
    freq, columns = 8, 6
    rows = 2 * freq
    dma = pltpu.SemaphoreType.DMA
    inputs = [jnp.transpose(snapshots, (1, 0, 2)), weights, bins]
    inputs = [pltpu.with_memory_space_constraint(value, pltpu.HBM) for value in inputs]
    values, gram = pl.pallas_call(
        functools.partial(kernel, space_count, lax.axis_size("var")),
        out_shape=(
            jax.ShapeDtypeStruct((columns, variables, freq, cells), jnp.float32),
            jax.ShapeDtypeStruct((freq, 128), jnp.float32),
        ),
        in_specs=[
            pl.BlockSpec(memory_space=pltpu.HBM),
            pl.BlockSpec(memory_space=pltpu.HBM),
            pl.BlockSpec(memory_space=pltpu.HBM),
        ],
        out_specs=(pl.BlockSpec(memory_space=pltpu.VMEM),) * 2,
        scratch_shapes=[
            pltpu.VMEM((variables, frames, cells), jnp.bfloat16),
            pltpu.VMEM((variables, cells), jnp.float32),
            pltpu.SMEM(bins.shape, jnp.int32),
            pltpu.VMEM((variables, rows, cells), jnp.float32),
            pltpu.VMEM((variables, 2 * rows, cells), jnp.bfloat16),
            pltpu.VMEM((variables, 2 * rows, cells), jnp.bfloat16),
            pltpu.VMEM((space_count, freq, 128), jnp.float32),
            dma((variables,)), dma, dma,
            dma((variables,)), dma((variables,)),
            dma((space_count - 1,)), dma((space_count - 1,)),
            pltpu.SemaphoreType.REGULAR,
        ],
        compiler_params=pltpu.CompilerParams(
            collective_id=0, has_side_effects=True, vmem_limit_bytes=32 * 1024 * 1024),
    )(*inputs)
    modes, factor = pl.pallas_call(
        functools.partial(modes_kernel, space_count),
        out_shape=(
            jax.ShapeDtypeStruct((columns, variables, freq, cells), jnp.float32),
            jax.ShapeDtypeStruct((columns, freq, columns), jnp.float32),
        ),
        in_specs=[pl.BlockSpec(memory_space=pltpu.VMEM)] * 2,
        out_specs=(pl.BlockSpec(memory_space=pltpu.HBM),) * 2,
        scratch_shapes=[
            pltpu.VMEM((columns, variables, freq, cells), jnp.float32),
            pltpu.VMEM((columns, freq, columns), jnp.float32),
            dma((columns,)), dma,
        ],
        compiler_params=pltpu.CompilerParams(vmem_limit_bytes=16 * 1024 * 1024),
    )(values, gram)
    return jnp.transpose(modes, (2, 0, 1, 3)), jnp.transpose(factor, (1, 0, 2))


def on_device(snapshots, weights, bins):
    seg_count = lax.axis_size("seg")
    var_count = lax.axis_size("var")
    space_count = lax.axis_size("space")
    frames, variables, cell_dev = snapshots.shape
    flat_rows = variables * cell_dev
    hop_len = frames // 2
    block_count = 2 * seg_count - 1
    freq_dev = bins.shape[0] // (seg_count * var_count)
    own = snapshots.reshape(frames, flat_rows)
    start_bin = (lax.axis_index("seg") * var_count + lax.axis_index("var")) * freq_dev
    chosen = lax.dynamic_slice_in_dim(bins, start_bin, freq_dev)
    piece = lax.all_gather(own, "seg", axis=0, tiled=True)
    count = piece.shape[0]
    moments = jnp.arange(count, dtype=jnp.int32)
    offset = moments[:, None] - hop_len * jnp.arange(block_count, dtype=jnp.int32)[None, :]
    inside = (offset >= 0) & (offset < frames)
    safe_offset = jnp.where(inside, offset, 0)
    cosine, sine = window_basis(safe_offset[:, :, None], chosen[None, None, :], frames)
    coeffs = jnp.stack([cosine, sine], 3) * inside[:, :, None, None].astype(jnp.float32)
    coeffs = jnp.transpose(coeffs, (0, 2, 3, 1)).reshape(count, freq_dev * 2 * block_count)
    coeffs = coeffs.astype(jnp.bfloat16)
    summed = jnp.einsum("pk,pr->kr", coeffs, piece, preferred_element_type=jnp.float32)
    spectra = summed.astype(jnp.bfloat16).reshape(freq_dev, 2 * block_count, flat_rows)
    values = spectra.astype(jnp.float32)
    scaled = values * weights.reshape(flat_rows)
    local_gram = jnp.einsum("fir,fjr->fij", scaled, values, precision=lax.Precision.HIGHEST)
    local_gram = local_gram / (variables * cell_dev * space_count)
    lower = jnp.linalg.cholesky(lax.psum(local_gram, "space"))
    inverse = invert_lower(lower)
    modes = jnp.einsum("fij,fjr->fir", inverse, values, precision=lax.Precision.HIGHEST)
    modes = modes.reshape(freq_dev, 2 * block_count, variables, cell_dev)
    return (modes, jnp.swapaxes(lower, 1, 2))


def per_device(snapshots, weights, bins):
    seg_count = lax.axis_size("seg")
    frames, variables, cells = snapshots.shape
    freq_dev = bins.shape[0] // (seg_count * lax.axis_size("var"))
    fits = seg_count == 2 and lax.axis_size("var") == 2 and freq_dev == 8 and cells % 128 == 0
    fits = fits and frames >= 256 and frames & (frames - 1) == 0 and lax.axis_size("space") > 1
    return (on_device_kernel if fits else on_device)(snapshots, weights, bins)


def solution(mesh):
    return jax.shard_map(
        per_device,
        mesh=mesh,
        in_specs=(P(("grp", "seg"), None, "space"), P(None, ("grp", "space")), P()),
        out_specs=(
            P(("seg", "var"), None, None, ("grp", "space")),
            P(("grp", "seg", "var"), None, None),
        ),
        check_vma=False,
    )
```

```python
import functools
import math

import jax
import jax.numpy as jnp
from jax import lax
from jax.experimental import pallas as pl
from jax.experimental.pallas import tpu as pltpu
from jax.sharding import PartitionSpec as P


def window_basis(offset, bin_index, length):
    phase = offset * bin_index % length
    angle = 2.0 * math.pi / length * phase.astype(jnp.float32)
    taper = 0.5 - 0.5 * jnp.cos(2.0 * math.pi / length * offset.astype(jnp.float32))
    factor = taper / math.sqrt(0.375 * length)
    return (factor * jnp.cos(angle), -factor * jnp.sin(angle))


def invert_lower(lower):
    identity = jnp.eye(lower.shape[-1], dtype=lower.dtype)

    def solve_single(single):
        return jax.scipy.linalg.solve_triangular(single, identity, lower=True)

    return jax.vmap(solve_single)(lower)


MESH = pl.DeviceIdType.MESH


def cosine_of(phase, length):
    quarter = jnp.abs(phase - length // 2) - length // 4
    x = quarter.astype(jnp.float32) * (2.0 * math.pi / length)
    y = x * x
    poly = -1.0 / 39916800.0
    for term in (1.0 / 362880.0, -1.0 / 5040.0, 1.0 / 120.0, -1.0 / 6.0, 1.0):
        poly = poly * y + term
    return x * poly


def basis_rows(bins_ref, frames, seg, var, var_count):
    freq = 8
    shape = (freq, frames)
    frame = lax.broadcasted_iota(jnp.int32, shape, 1)
    row = lax.broadcasted_iota(jnp.int32, shape, 0)
    half = frames // 2
    taper = (0.5 - 0.5 * cosine_of(frame, frames)) / math.sqrt(0.375 * frames)
    second = (lax.broadcasted_iota(jnp.int32, (2 * freq, frames), 1) >= half).astype(jnp.int32)
    overlap = second == 1 - seg
    rows = []
    for group in range(2):
        owner = 1 - seg if group == 0 else seg
        first = (owner * var_count + var) * freq
        bin_of = jnp.zeros(shape, jnp.int32)
        for f in range(freq):
            bin_of = jnp.where(row == f, bins_ref[first + f], bin_of)
        phase = (frame * bin_of) & (frames - 1)
        cosine = taper * cosine_of(phase, frames)
        sine = taper * cosine_of((phase + frames // 4) & (frames - 1), frames)
        whole = jnp.concatenate([cosine, sine], 0)
        shared = jnp.concatenate([whole[:, half:], whole[:, :half]], 1)
        rows += [whole, jnp.where(overlap, shared, 0.0)]
    return jnp.concatenate(rows, 0).astype(jnp.bfloat16)


def kernel(space_count, var_count, x_hbm, w_hbm, bins_hbm, values, gram_ref,
           x_vmem, w_ref, bins_ref, own_half, send, recv, gram_buf,
           x_sem, w_sem, bins_sem, send_sem, recv_sem, g_send_sem, g_recv_sem, turn_sem):
    variables, frames, cells = x_hbm.shape
    freq = 8
    rows = 2 * freq
    seg = lax.axis_index("seg")
    var = lax.axis_index("var")
    me = lax.axis_index("space")
    other = 1 - seg
    bins_load = pltpu.make_async_copy(bins_hbm, bins_ref, bins_sem)
    bins_load.start()
    for v in range(variables):
        pltpu.make_async_copy(x_hbm.at[v], x_vmem.at[v], x_sem.at[v]).start()

    w_load = pltpu.make_async_copy(w_hbm, w_ref, w_sem)
    w_load.start()

    barrier = pltpu.get_barrier_semaphore()
    pl.semaphore_signal(barrier, inc=1, device_id={"seg": other}, device_id_type=MESH)
    pl.semaphore_signal(barrier, inc=1, device_id={"var": 1 - var}, device_id_type=MESH)
    for d in range(1, space_count):
        pl.semaphore_signal(
            barrier, inc=1, device_id={"space": lax.rem(me + d, space_count)}, device_id_type=MESH)

    bins_load.wait()
    basis = basis_rows(bins_ref, frames, seg, var, var_count)

    pl.semaphore_wait(barrier, space_count + 1)
    early = 1
    copies = [
        pltpu.make_async_remote_copy(
            src_ref=send.at[v], dst_ref=recv.at[v], send_sem=send_sem.at[v], recv_sem=recv_sem.at[v],
            device_id={"seg": other}, device_id_type=MESH)
        for v in range(variables)]

    def transform(v, start=None):
        pltpu.make_async_copy(x_hbm.at[v], x_vmem.at[v], x_sem.at[v]).wait()
        summed = jnp.dot(basis, x_vmem[v], preferred_element_type=jnp.float32)
        send[v] = summed[:2 * rows].astype(send.dtype)
        if start is not None:
            start()
        own = summed[2 * rows:3 * rows].astype(jnp.bfloat16).astype(jnp.float32)
        own_half[v] = summed[3 * rows:]
        for part in range(2):
            values[3 * part + 2 * seg, v] = own[part * freq:(part + 1) * freq]

    @pl.when(var == 0)
    def _():
        for v in range(variables):
            transform(v, copies[v].start)
        for copy in copies[:early]:
            copy.wait_send()
        pl.semaphore_signal(turn_sem, inc=1, device_id={"var": 1 - var}, device_id_type=MESH)

    @pl.when(var != 0)
    def _():
        pl.loop(0, variables)(transform)
        pl.semaphore_wait(turn_sem, 1)
        for copy in copies:
            copy.start()

    w_load.wait()
    columns = 6
    pairs = [(i, j) for i in range(columns) for j in range(i + 1)]
    sums = tuple(jnp.zeros((freq, 128), jnp.float32) for _ in pairs)
    for v in range(variables):
        copies[v].wait_recv()
        far = recv[v].astype(jnp.float32)
        total = own_half[v] + far[rows:]
        total = total.astype(jnp.bfloat16).astype(jnp.float32)
        for part in range(2):
            values[3 * part + 1, v] = total[part * freq:(part + 1) * freq]
            values[3 * part + 2 * other, v] = far[part * freq:(part + 1) * freq]
        def add_block(block, sums, v=v):
            one = pl.ds(pl.multiple_of(block * 128, 128), 128)
            weight = jnp.broadcast_to(w_ref[v:v + 1, one], (freq, 128))
            plain = [values[i, v, :, one] for i in range(columns)]
            scaled = [p * weight for p in plain]
            return tuple(
                total + scaled[i] * plain[j] for total, (i, j) in zip(sums, pairs))

        sums = lax.fori_loop(0, cells // 128, add_block, sums)

    lane = lax.broadcasted_iota(jnp.int32, (freq, 128), 1)
    packed = jnp.zeros((freq, 128), jnp.float32)
    for n in range(len(pairs)):
        packed = jnp.where(lane == n, jnp.sum(sums[n], axis=1, keepdims=True), packed)
    gram_buf[me] = packed
    g_copies = []
    for d in range(1, space_count):
        copy = pltpu.make_async_remote_copy(
            src_ref=gram_buf.at[me], dst_ref=gram_buf.at[me],
            send_sem=g_send_sem.at[d - 1], recv_sem=g_recv_sem.at[d - 1],
            device_id={"space": lax.rem(me + d, space_count)}, device_id_type=MESH)
        copy.start()
        g_copies.append(copy)
    for copy in g_copies:
        copy.wait_recv()
    gram = gram_buf[0]
    for d in range(1, space_count):
        gram = gram + gram_buf[d]
    gram_ref[...] = gram

    @pl.when(var != 0)
    def _():
        for copy in copies[:early]:
            copy.wait_send()

    for copy in copies[early:] + g_copies:
        copy.wait_send()


def modes_kernel(space_count, values, gram_ref, modes_hbm, factor_hbm, modes_vmem, factor_ref, modes_sem, factor_sem):
    columns, variables, freq, cells = values.shape
    pairs = [(i, j) for i in range(columns) for j in range(i + 1)]
    lane = lax.broadcasted_iota(jnp.int32, (freq, 128), 1)
    gram = gram_ref[...] * (1.0 / (variables * cells * space_count))
    entry = {
        pair: jnp.broadcast_to(gram[:, n:n + 1], (freq, 128)) for n, pair in enumerate(pairs)}

    lower, inverse = {}, {}
    for j in range(columns):
        rest = entry[j, j]
        for k in range(j):
            rest = rest - lower[j, k] * lower[j, k]
        inverse[j, j] = lax.rsqrt(rest)
        lower[j, j] = rest * inverse[j, j]
        for i in range(j + 1, columns):
            rest = entry[i, j]
            for k in range(j):
                rest = rest - lower[i, k] * lower[j, k]
            lower[i, j] = rest * inverse[j, j]
    for j in range(columns):
        for i in range(j + 1, columns):
            total = lower[i, j] * inverse[j, j]
            for k in range(j + 1, i):
                total = total + lower[i, k] * inverse[k, j]
            inverse[i, j] = -total * inverse[i, i]

    for i in range(columns):
        line = jnp.zeros((freq, 128), jnp.float32)
        for j in range(i, columns):
            line = jnp.where(lane == j, lower[j, i], line)
        factor_ref[i] = line[:, :columns]

    copies = [pltpu.make_async_copy(factor_ref, factor_hbm, factor_sem)]
    copies[0].start()
    for i in range(columns):
        for v in range(variables):
            for at in range(0, cells, 128):
                one = pl.ds(at, 128)
                mode = inverse[i, 0] * values[0, v, :, one]
                for j in range(1, i + 1):
                    mode = mode + inverse[i, j] * values[j, v, :, one]
                modes_vmem[i, v, :, one] = mode
        copy = pltpu.make_async_copy(modes_vmem.at[i], modes_hbm.at[i], modes_sem.at[i])
        copy.start()
        copies.append(copy)
    for copy in copies:
        copy.wait()


def on_device_kernel(snapshots, weights, bins):
    frames, variables, cells = snapshots.shape
    space_count = lax.axis_size("space")
    freq, columns = 8, 6
    rows = 2 * freq
    dma = pltpu.SemaphoreType.DMA
    inputs = [jnp.transpose(snapshots, (1, 0, 2)), weights, bins]
    inputs = [pltpu.with_memory_space_constraint(value, pltpu.HBM) for value in inputs]
    values, gram = pl.pallas_call(
        functools.partial(kernel, space_count, lax.axis_size("var")),
        out_shape=(
            jax.ShapeDtypeStruct((columns, variables, freq, cells), jnp.float32),
            jax.ShapeDtypeStruct((freq, 128), jnp.float32),
        ),
        in_specs=[
            pl.BlockSpec(memory_space=pltpu.HBM),
            pl.BlockSpec(memory_space=pltpu.HBM),
            pl.BlockSpec(memory_space=pltpu.HBM),
        ],
        out_specs=(pl.BlockSpec(memory_space=pltpu.VMEM),) * 2,
        scratch_shapes=[
            pltpu.VMEM((variables, frames, cells), jnp.bfloat16),
            pltpu.VMEM((variables, cells), jnp.float32),
            pltpu.SMEM(bins.shape, jnp.int32),
            pltpu.VMEM((variables, rows, cells), jnp.float32),
            pltpu.VMEM((variables, 2 * rows, cells), jnp.bfloat16),
            pltpu.VMEM((variables, 2 * rows, cells), jnp.bfloat16),
            pltpu.VMEM((space_count, freq, 128), jnp.float32),
            dma((variables,)), dma, dma,
            dma((variables,)), dma((variables,)),
            dma((space_count - 1,)), dma((space_count - 1,)),
            pltpu.SemaphoreType.REGULAR,
        ],
        compiler_params=pltpu.CompilerParams(
            collective_id=0, has_side_effects=True, vmem_limit_bytes=32 * 1024 * 1024),
    )(*inputs)
    modes, factor = pl.pallas_call(
        functools.partial(modes_kernel, space_count),
        out_shape=(
            jax.ShapeDtypeStruct((columns, variables, freq, cells), jnp.float32),
            jax.ShapeDtypeStruct((columns, freq, columns), jnp.float32),
        ),
        in_specs=[pl.BlockSpec(memory_space=pltpu.VMEM)] * 2,
        out_specs=(pl.BlockSpec(memory_space=pltpu.HBM),) * 2,
        scratch_shapes=[
            pltpu.VMEM((columns, variables, freq, cells), jnp.float32),
            pltpu.VMEM((columns, freq, columns), jnp.float32),
            dma((columns,)), dma,
        ],
        compiler_params=pltpu.CompilerParams(vmem_limit_bytes=16 * 1024 * 1024),
    )(values, gram)
    return jnp.transpose(modes, (2, 0, 1, 3)), jnp.transpose(factor, (1, 0, 2))


def on_device(snapshots, weights, bins):
    seg_count = lax.axis_size("seg")
    var_count = lax.axis_size("var")
    space_count = lax.axis_size("space")
    frames, variables, cell_dev = snapshots.shape
    flat_rows = variables * cell_dev
    hop_len = frames // 2
    block_count = 2 * seg_count - 1
    freq_dev = bins.shape[0] // (seg_count * var_count)
    own = snapshots.reshape(frames, flat_rows)
    start_bin = (lax.axis_index("seg") * var_count + lax.axis_index("var")) * freq_dev
    chosen = lax.dynamic_slice_in_dim(bins, start_bin, freq_dev)
    piece = lax.all_gather(own, "seg", axis=0, tiled=True)
    count = piece.shape[0]
    moments = jnp.arange(count, dtype=jnp.int32)
    offset = moments[:, None] - hop_len * jnp.arange(block_count, dtype=jnp.int32)[None, :]
    inside = (offset >= 0) & (offset < frames)
    safe_offset = jnp.where(inside, offset, 0)
    cosine, sine = window_basis(safe_offset[:, :, None], chosen[None, None, :], frames)
    coeffs = jnp.stack([cosine, sine], 3) * inside[:, :, None, None].astype(jnp.float32)
    coeffs = jnp.transpose(coeffs, (0, 2, 3, 1)).reshape(count, freq_dev * 2 * block_count)
    coeffs = coeffs.astype(jnp.bfloat16)
    summed = jnp.einsum("pk,pr->kr", coeffs, piece, preferred_element_type=jnp.float32)
    spectra = summed.astype(jnp.bfloat16).reshape(freq_dev, 2 * block_count, flat_rows)
    values = spectra.astype(jnp.float32)
    scaled = values * weights.reshape(flat_rows)
    local_gram = jnp.einsum("fir,fjr->fij", scaled, values, precision=lax.Precision.HIGHEST)
    local_gram = local_gram / (variables * cell_dev * space_count)
    lower = jnp.linalg.cholesky(lax.psum(local_gram, "space"))
    inverse = invert_lower(lower)
    modes = jnp.einsum("fij,fjr->fir", inverse, values, precision=lax.Precision.HIGHEST)
    modes = modes.reshape(freq_dev, 2 * block_count, variables, cell_dev)
    return (modes, jnp.swapaxes(lower, 1, 2))


def per_device(snapshots, weights, bins):
    seg_count = lax.axis_size("seg")
    frames, variables, cells = snapshots.shape
    freq_dev = bins.shape[0] // (seg_count * lax.axis_size("var"))
    fits = seg_count == 2 and lax.axis_size("var") == 2 and freq_dev == 8 and cells % 128 == 0
    fits = fits and frames >= 256 and frames & (frames - 1) == 0 and lax.axis_size("space") > 1
    return (on_device_kernel if fits else on_device)(snapshots, weights, bins)


def solution(mesh):
    return jax.shard_map(
        per_device,
        mesh=mesh,
        in_specs=(P(("grp", "seg"), None, "space"), P(None, ("grp", "space")), P()),
        out_specs=(
            P(("seg", "var"), None, None, ("grp", "space")),
            P(("grp", "seg", "var"), None, None),
        ),
        check_vma=False,
    )
```

```python
import functools
import math

import jax
import jax.numpy as jnp
from jax import lax
from jax.experimental import pallas as pl
from jax.experimental.pallas import tpu as pltpu
from jax.sharding import PartitionSpec as P


def window_basis(offset, bin_index, length):
    phase = offset * bin_index % length
    angle = 2.0 * math.pi / length * phase.astype(jnp.float32)
    taper = 0.5 - 0.5 * jnp.cos(2.0 * math.pi / length * offset.astype(jnp.float32))
    factor = taper / math.sqrt(0.375 * length)
    return (factor * jnp.cos(angle), -factor * jnp.sin(angle))


def invert_lower(lower):
    identity = jnp.eye(lower.shape[-1], dtype=lower.dtype)

    def solve_single(single):
        return jax.scipy.linalg.solve_triangular(single, identity, lower=True)

    return jax.vmap(solve_single)(lower)


MESH = pl.DeviceIdType.MESH


def cosine_of(phase, length):
    quarter = jnp.abs(phase - length // 2) - length // 4
    x = quarter.astype(jnp.float32) * (2.0 * math.pi / length)
    y = x * x
    poly = -1.0 / 39916800.0
    for term in (1.0 / 362880.0, -1.0 / 5040.0, 1.0 / 120.0, -1.0 / 6.0, 1.0):
        poly = poly * y + term
    return x * poly


def basis_rows(bins_ref, frames, seg, var, var_count):
    freq = 8
    shape = (freq, frames)
    frame = lax.broadcasted_iota(jnp.int32, shape, 1)
    row = lax.broadcasted_iota(jnp.int32, shape, 0)
    half = frames // 2
    taper = (0.5 - 0.5 * cosine_of(frame, frames)) / math.sqrt(0.375 * frames)
    second = (lax.broadcasted_iota(jnp.int32, (2 * freq, frames), 1) >= half).astype(jnp.int32)
    overlap = second == 1 - seg
    rows = []
    for group in range(2):
        owner = 1 - seg if group == 0 else seg
        first = (owner * var_count + var) * freq
        bin_of = jnp.zeros(shape, jnp.int32)
        for f in range(freq):
            bin_of = jnp.where(row == f, bins_ref[first + f], bin_of)
        phase = (frame * bin_of) & (frames - 1)
        cosine = taper * cosine_of(phase, frames)
        sine = taper * cosine_of((phase + frames // 4) & (frames - 1), frames)
        whole = jnp.concatenate([cosine, sine], 0)
        shared = jnp.concatenate([whole[:, half:], whole[:, :half]], 1)
        rows += [whole, jnp.where(overlap, shared, 0.0)]
    return jnp.concatenate(rows, 0).astype(jnp.bfloat16)


def kernel(space_count, var_count, x_hbm, w_hbm, bins_hbm, values, gram_ref,
           x_vmem, w_ref, bins_ref, own_half, send, recv, gram_buf,
           x_sem, w_sem, bins_sem, send_sem, recv_sem, g_send_sem, g_recv_sem, turn_sem):
    variables, frames, cells = x_hbm.shape
    freq = 8
    rows = 2 * freq
    seg = lax.axis_index("seg")
    var = lax.axis_index("var")
    me = lax.axis_index("space")
    other = 1 - seg
    bins_load = pltpu.make_async_copy(bins_hbm, bins_ref, bins_sem)
    bins_load.start()
    loads = []
    for v in range(variables):
        load = pltpu.make_async_copy(x_hbm.at[v], x_vmem.at[v], x_sem.at[v])
        load.start()
        loads.append(load)

    w_load = pltpu.make_async_copy(w_hbm, w_ref, w_sem)
    w_load.start()

    barrier = pltpu.get_barrier_semaphore()
    pl.semaphore_signal(barrier, inc=1, device_id={"seg": other}, device_id_type=MESH)
    pl.semaphore_signal(barrier, inc=1, device_id={"var": 1 - var}, device_id_type=MESH)
    for d in range(1, space_count):
        pl.semaphore_signal(
            barrier, inc=1, device_id={"space": lax.rem(me + d, space_count)}, device_id_type=MESH)

    bins_load.wait()
    basis = basis_rows(bins_ref, frames, seg, var, var_count)

    pl.semaphore_wait(barrier, space_count + 1)
    early = 2
    copies = [
        pltpu.make_async_remote_copy(
            src_ref=send.at[v], dst_ref=recv.at[v], send_sem=send_sem.at[v], recv_sem=recv_sem.at[v],
            device_id={"seg": other}, device_id_type=MESH)
        for v in range(variables)]

    def transform(v, start=None):
        loads[v].wait()
        summed = jnp.dot(basis, x_vmem[v], preferred_element_type=jnp.float32)
        send[v] = summed[:2 * rows].astype(send.dtype)
        if start is not None:
            start()
        own = summed[2 * rows:3 * rows].astype(jnp.bfloat16).astype(jnp.float32)
        own_half[v] = summed[3 * rows:]
        for part in range(2):
            values[3 * part + 2 * seg, v] = own[part * freq:(part + 1) * freq]

    @pl.when(var == 0)
    def _():
        for v in range(variables):
            transform(v, copies[v].start)
        for copy in copies[:early]:
            copy.wait_send()
        pl.semaphore_signal(turn_sem, inc=1, device_id={"var": 1 - var}, device_id_type=MESH)

    @pl.when(var != 0)
    def _():
        for v in range(variables):
            transform(v)
        pl.semaphore_wait(turn_sem, 1)
        for copy in copies:
            copy.start()

    w_load.wait()
    columns = 6
    pairs = [(i, j) for i in range(columns) for j in range(i + 1)]
    sums = [None] * len(pairs)
    for v in range(variables):
        copies[v].wait_recv()
        far = recv[v].astype(jnp.float32)
        total = own_half[v] + far[rows:]
        total = total.astype(jnp.bfloat16).astype(jnp.float32)
        for part in range(2):
            values[3 * part + 1, v] = total[part * freq:(part + 1) * freq]
            values[3 * part + 2 * other, v] = far[part * freq:(part + 1) * freq]
        for at in range(0, cells, 128):
            one = pl.ds(at, 128)
            weight = jnp.broadcast_to(w_ref[v:v + 1, one], (freq, 128))
            plain = [values[i, v, :, one] for i in range(columns)]
            scaled = [p * weight for p in plain]
            for n, (i, j) in enumerate(pairs):
                term = scaled[i] * plain[j]
                sums[n] = term if sums[n] is None else sums[n] + term

    lane = lax.broadcasted_iota(jnp.int32, (freq, 128), 1)
    packed = jnp.zeros((freq, 128), jnp.float32)
    for n in range(len(pairs)):
        packed = jnp.where(lane == n, jnp.sum(sums[n], axis=1, keepdims=True), packed)
    gram_buf[me] = packed
    g_copies = []
    for d in range(1, space_count):
        copy = pltpu.make_async_remote_copy(
            src_ref=gram_buf.at[me], dst_ref=gram_buf.at[me],
            send_sem=g_send_sem.at[d - 1], recv_sem=g_recv_sem.at[d - 1],
            device_id={"space": lax.rem(me + d, space_count)}, device_id_type=MESH)
        copy.start()
        g_copies.append(copy)
    for copy in g_copies:
        copy.wait_recv()
    gram = gram_buf[0]
    for d in range(1, space_count):
        gram = gram + gram_buf[d]
    gram_ref[...] = gram

    @pl.when(var != 0)
    def _():
        for copy in copies[:early]:
            copy.wait_send()

    for copy in copies[early:] + g_copies:
        copy.wait_send()


def modes_kernel(space_count, values, gram_ref, modes_hbm, factor_hbm, modes_vmem, factor_ref, modes_sem, factor_sem):
    columns, variables, freq, cells = values.shape
    pairs = [(i, j) for i in range(columns) for j in range(i + 1)]
    lane = lax.broadcasted_iota(jnp.int32, (freq, 128), 1)
    gram = gram_ref[...] * (1.0 / (variables * cells * space_count))
    entry = {
        pair: jnp.broadcast_to(gram[:, n:n + 1], (freq, 128)) for n, pair in enumerate(pairs)}

    lower, inverse = {}, {}
    for j in range(columns):
        rest = entry[j, j]
        for k in range(j):
            rest = rest - lower[j, k] * lower[j, k]
        inverse[j, j] = lax.rsqrt(rest)
        lower[j, j] = rest * inverse[j, j]
        for i in range(j + 1, columns):
            rest = entry[i, j]
            for k in range(j):
                rest = rest - lower[i, k] * lower[j, k]
            lower[i, j] = rest * inverse[j, j]
    for j in range(columns):
        for i in range(j + 1, columns):
            total = lower[i, j] * inverse[j, j]
            for k in range(j + 1, i):
                total = total + lower[i, k] * inverse[k, j]
            inverse[i, j] = -total * inverse[i, i]

    for i in range(columns):
        line = jnp.zeros((freq, 128), jnp.float32)
        for j in range(i, columns):
            line = jnp.where(lane == j, lower[j, i], line)
        factor_ref[i] = line[:, :columns]

    copies = [pltpu.make_async_copy(factor_ref, factor_hbm, factor_sem)]
    copies[0].start()
    for i in range(columns):
        for v in range(variables):
            for at in range(0, cells, 128):
                one = pl.ds(at, 128)
                mode = inverse[i, 0] * values[0, v, :, one]
                for j in range(1, i + 1):
                    mode = mode + inverse[i, j] * values[j, v, :, one]
                modes_vmem[i, v, :, one] = mode
        copy = pltpu.make_async_copy(modes_vmem.at[i], modes_hbm.at[i], modes_sem.at[i])
        copy.start()
        copies.append(copy)
    for copy in copies:
        copy.wait()


def on_device_kernel(snapshots, weights, bins):
    frames, variables, cells = snapshots.shape
    space_count = lax.axis_size("space")
    freq, columns = 8, 6
    rows = 2 * freq
    dma = pltpu.SemaphoreType.DMA
    inputs = [jnp.transpose(snapshots, (1, 0, 2)), weights, bins]
    inputs = [pltpu.with_memory_space_constraint(value, pltpu.HBM) for value in inputs]
    values, gram = pl.pallas_call(
        functools.partial(kernel, space_count, lax.axis_size("var")),
        out_shape=(
            jax.ShapeDtypeStruct((columns, variables, freq, cells), jnp.float32),
            jax.ShapeDtypeStruct((freq, 128), jnp.float32),
        ),
        in_specs=[
            pl.BlockSpec(memory_space=pltpu.HBM),
            pl.BlockSpec(memory_space=pltpu.HBM),
            pl.BlockSpec(memory_space=pltpu.HBM),
        ],
        out_specs=(pl.BlockSpec(memory_space=pltpu.VMEM),) * 2,
        scratch_shapes=[
            pltpu.VMEM((variables, frames, cells), jnp.bfloat16),
            pltpu.VMEM((variables, cells), jnp.float32),
            pltpu.SMEM(bins.shape, jnp.int32),
            pltpu.VMEM((variables, rows, cells), jnp.float32),
            pltpu.VMEM((variables, 2 * rows, cells), jnp.bfloat16),
            pltpu.VMEM((variables, 2 * rows, cells), jnp.bfloat16),
            pltpu.VMEM((space_count, freq, 128), jnp.float32),
            dma((variables,)), dma, dma,
            dma((variables,)), dma((variables,)),
            dma((space_count - 1,)), dma((space_count - 1,)),
            pltpu.SemaphoreType.REGULAR,
        ],
        compiler_params=pltpu.CompilerParams(
            collective_id=0, has_side_effects=True, vmem_limit_bytes=32 * 1024 * 1024),
    )(*inputs)
    modes, factor = pl.pallas_call(
        functools.partial(modes_kernel, space_count),
        out_shape=(
            jax.ShapeDtypeStruct((columns, variables, freq, cells), jnp.float32),
            jax.ShapeDtypeStruct((columns, freq, columns), jnp.float32),
        ),
        in_specs=[pl.BlockSpec(memory_space=pltpu.VMEM)] * 2,
        out_specs=(pl.BlockSpec(memory_space=pltpu.HBM),) * 2,
        scratch_shapes=[
            pltpu.VMEM((columns, variables, freq, cells), jnp.float32),
            pltpu.VMEM((columns, freq, columns), jnp.float32),
            dma((columns,)), dma,
        ],
        compiler_params=pltpu.CompilerParams(vmem_limit_bytes=16 * 1024 * 1024),
    )(values, gram)
    return jnp.transpose(modes, (2, 0, 1, 3)), jnp.transpose(factor, (1, 0, 2))


def on_device(snapshots, weights, bins):
    seg_count = lax.axis_size("seg")
    var_count = lax.axis_size("var")
    space_count = lax.axis_size("space")
    frames, variables, cell_dev = snapshots.shape
    flat_rows = variables * cell_dev
    hop_len = frames // 2
    block_count = 2 * seg_count - 1
    freq_dev = bins.shape[0] // (seg_count * var_count)
    own = snapshots.reshape(frames, flat_rows)
    start_bin = (lax.axis_index("seg") * var_count + lax.axis_index("var")) * freq_dev
    chosen = lax.dynamic_slice_in_dim(bins, start_bin, freq_dev)
    piece = lax.all_gather(own, "seg", axis=0, tiled=True)
    count = piece.shape[0]
    moments = jnp.arange(count, dtype=jnp.int32)
    offset = moments[:, None] - hop_len * jnp.arange(block_count, dtype=jnp.int32)[None, :]
    inside = (offset >= 0) & (offset < frames)
    safe_offset = jnp.where(inside, offset, 0)
    cosine, sine = window_basis(safe_offset[:, :, None], chosen[None, None, :], frames)
    coeffs = jnp.stack([cosine, sine], 3) * inside[:, :, None, None].astype(jnp.float32)
    coeffs = jnp.transpose(coeffs, (0, 2, 3, 1)).reshape(count, freq_dev * 2 * block_count)
    coeffs = coeffs.astype(jnp.bfloat16)
    summed = jnp.einsum("pk,pr->kr", coeffs, piece, preferred_element_type=jnp.float32)
    spectra = summed.astype(jnp.bfloat16).reshape(freq_dev, 2 * block_count, flat_rows)
    values = spectra.astype(jnp.float32)
    scaled = values * weights.reshape(flat_rows)
    local_gram = jnp.einsum("fir,fjr->fij", scaled, values, precision=lax.Precision.HIGHEST)
    local_gram = local_gram / (variables * cell_dev * space_count)
    lower = jnp.linalg.cholesky(lax.psum(local_gram, "space"))
    inverse = invert_lower(lower)
    modes = jnp.einsum("fij,fjr->fir", inverse, values, precision=lax.Precision.HIGHEST)
    modes = modes.reshape(freq_dev, 2 * block_count, variables, cell_dev)
    return (modes, jnp.swapaxes(lower, 1, 2))


def per_device(snapshots, weights, bins):
    seg_count = lax.axis_size("seg")
    frames, variables, cells = snapshots.shape
    freq_dev = bins.shape[0] // (seg_count * lax.axis_size("var"))
    fits = seg_count == 2 and lax.axis_size("var") == 2 and freq_dev == 8 and cells % 128 == 0
    fits = fits and frames >= 256 and frames & (frames - 1) == 0 and lax.axis_size("space") > 1
    return (on_device_kernel if fits else on_device)(snapshots, weights, bins)


def solution(mesh):
    return jax.shard_map(
        per_device,
        mesh=mesh,
        in_specs=(P(("grp", "seg"), None, "space"), P(None, ("grp", "space")), P()),
        out_specs=(
            P(("seg", "var"), None, None, ("grp", "space")),
            P(("grp", "seg", "var"), None, None),
        ),
        check_vma=False,
    )
```
